32 devices in a mesh: row: 2 (over core), col: 16 (over z, y, x).
Axes of the slice: x: 2, y: 2, z: 4, core: 2. Of those that a mesh axis runs over, the one named last changes fastest.
Arguments:
- features: bfloat16 [512, 8192], P('col', 'row'), may hold values from -6 to 6
- a_blocks: bfloat16 [64, 2, 2, 128, 128], P('row'), may hold values from -0.375 to 0.375
- block_cols: int32 [64, 2, 2], P('row'), may hold values from 0 to 31
- block_counts: int32 [64, 2], P('row'), may hold values from 0 to 2
- weight: bfloat16 [512, 512], P('col'), may hold values from -0.25 to 0.25
- cotangent: bfloat16 [512, 8192], P('col', 'row'), may hold values from -6 to 6
Outputs:
- output: bfloat16 [512, 8192], P('col', 'row')
- grad_weight: float32 [512, 512], P('col')
- grad_features: bfloat16 [512, 8192], P('col', 'row')
The draws below stay inside these ranges and needn't reach their ends.
Inputs may be any that keep to these rules, and one draw needn't show every extreme that they name: `block_cols`: block column indices lie within one slab's blocks.
All inputs are finite; a program needn't handle non-finite values.
Results may differ from the reference program's by a relative error of at most 0.0061.
Values may be sent and summed in bfloat16 or wider, within the bound.
A program may use at most 128 MiB of HBM per device.

```python
import jax
import jax.numpy as jnp
from jax import lax

F = 512
BLOCK = 128
KB = 2
ROWS_DEV = 4096
SECTIONS = 2
NODES = 8192
NBLOCKS = 64


def with_ends(values, key, least, high):
    extent = values.shape
    spot = [jax.random.randint(jax.random.fold_in(key, axis), (), 0, extent[axis]) for axis in range(len(extent))]
    values = values.at[tuple(spot)].set(least)
    longest = extent.index(max(extent))
    spot[longest] = (spot[longest] + 1) % extent[longest]
    return values.at[tuple(spot)].set(high)


def steps_of(stream_key, extent, shards, low, top_value):
    def one(axis_at, blocks):
        steps = jax.random.uniform(jax.random.fold_in(jax.random.fold_in(stream_key, 6), axis_at), (blocks,), jnp.float32, low / len(shards), top_value / len(shards))
        return jnp.repeat(jnp.exp(steps), extent[axis_at] // blocks).reshape((-1,) + (1,) * (len(extent) - axis_at - 1))

    level = one(*shards[0])
    for cut in shards[1:]:
        level = level * one(*cut)
    return level


def gaussian(stream_key, extent, width, limit, pieces=(), held_as=jnp.bfloat16):
    loudness = steps_of(stream_key, extent, pieces, -0.22, 0.18) if pieces else 1.0
    result = jax.random.normal(stream_key, extent, jnp.float32) * width * loudness
    return jnp.minimum(jnp.maximum(result, -limit), limit).astype(held_as)


def setup_inputs(seed: int = 0) -> dict:
    key_of = jax.random.split(jax.random.key(seed), 7)
    features = gaussian(key_of[0], (F, NODES), 1.0, 6.0, ((0, 16), (1, 2)))
    a_blocks = gaussian(key_of[1], (NBLOCKS, SECTIONS, KB, BLOCK, BLOCK), (SECTIONS * KB * BLOCK // 2) ** -0.5, 0.375, ((0, 2),))
    block_cols = with_ends(jax.random.randint(key_of[2], (NBLOCKS, SECTIONS, KB), 0, ROWS_DEV // BLOCK), jax.random.fold_in(key_of[2], 1), 0, (ROWS_DEV // BLOCK) - 1).astype(jnp.int32)
    block_counts = with_ends(jax.random.randint(key_of[3], (NBLOCKS, SECTIONS), 0, KB + 1), jax.random.fold_in(key_of[3], 1), 0, KB).astype(jnp.int32)
    weight = gaussian(key_of[4], (F, F), F ** -0.5, 0.25, ((0, 16),))
    cotangent = gaussian(key_of[5], (F, NODES), 1.0, 6.0, ((0, 16), (1, 2)))
    return {"features": features, "a_blocks": a_blocks, "block_cols": block_cols, "block_counts": block_counts, "weight": weight, "cotangent": cotangent}


def reference(features, a_blocks, block_cols, block_counts, weight, cotangent):
    row_blocks = ROWS_DEV // BLOCK
    all_blocks = NODES // BLOCK
    global_index = (jnp.arange(SECTIONS, dtype=jnp.int32)[None, :, None] * row_blocks + block_cols).astype(jnp.int32)
    slot_ids = jnp.arange(KB, dtype=jnp.int32)
    panels = features.reshape(F, all_blocks, BLOCK).astype(jnp.float32)

    def masked_of(blocks, counts):
        live_mask = (slot_ids[None, :] < counts[:, None]).astype(jnp.float32)
        return blocks.astype(jnp.float32) * live_mask[:, :, None, None]

    def forward_one(packed):
        blocks, index_one, counts = packed
        picked = panels[:, index_one]
        return jnp.einsum('fskj,skij->fi', picked, masked_of(blocks, counts))
    gathered = lax.map(forward_one, (a_blocks, global_index, block_counts))
    aggregated = jnp.transpose(gathered, (1, 0, 2)).reshape(F, NODES).astype(jnp.bfloat16)
    preact = jnp.dot(weight, aggregated, preferred_element_type=jnp.float32)
    output = jax.nn.silu(preact).astype(jnp.bfloat16)
    sigmoid_pre = jax.nn.sigmoid(preact)
    dpre = (cotangent.astype(jnp.float32) * sigmoid_pre * (1.0 + preact * (1.0 - sigmoid_pre))).astype(jnp.bfloat16)
    grad_weight = lax.dot_general(dpre, aggregated, (((1,), (1,)), ((), ())), preferred_element_type=jnp.float32)
    grad_weight = grad_weight / jnp.sqrt(jnp.float32(NODES))
    dagg = lax.dot_general(weight, dpre, (((0,), (0,)), ((), ())), preferred_element_type=jnp.float32).astype(jnp.bfloat16)
    dagg_blocks = jnp.transpose(dagg.reshape(F, all_blocks, BLOCK), (1, 0, 2)).astype(jnp.float32)

    def back_one(total, packed):
        blocks, index_one, counts, grad_rows = packed
        contrib = jnp.einsum('fi,skij->fskj', grad_rows, masked_of(blocks, counts))
        return (total.at[:, index_one].add(contrib), None)
    start_total = jnp.zeros((F, all_blocks, BLOCK), jnp.float32)
    total, unused = lax.scan(back_one, start_total, (a_blocks, global_index, block_counts, dagg_blocks))
    grad_features = total.reshape(F, NODES).astype(jnp.bfloat16)
    return (output, grad_weight, grad_features)
```

```python
import functools
import math

import jax
import jax.numpy as jnp
from jax import lax
from jax.experimental import pallas as pl
from jax.experimental.pallas import tpu as pltpu
from jax.sharding import PartitionSpec as P

MESH = pl.DeviceIdType.MESH
f32 = jnp.float32
bf16 = jnp.bfloat16


def from_root(value, axis, source):
    kept = jnp.where(lax.axis_index(axis) == source, value, 0).astype(value.dtype)
    return lax.psum(kept, axis)


def plain(features, a_blocks, block_cols, block_counts, weight, cotangent):
    feat_dev = features.shape[0]
    slab_rows = features.shape[1]
    block_size = a_blocks.shape[-1]
    local_blocks = a_blocks.shape[0]
    section_count = a_blocks.shape[1]
    slot_count = a_blocks.shape[2]
    row_blocks = slab_rows // block_size
    slot_ids = jnp.arange(slot_count, dtype=jnp.int32)
    live_mask = (slot_ids[None, None, :] < block_counts[:, :, None]).astype(jnp.bfloat16)
    masked = a_blocks * live_mask[:, :, :, None, None]
    global_index = (
        jnp.arange(section_count, dtype=jnp.int32)[None, :, None] * row_blocks + block_cols
    )
    node_total = slab_rows * lax.axis_size("row")
    total = jnp.zeros((feat_dev, local_blocks, block_size), jnp.float32)
    for section_idx in range(lax.axis_size("row")):
        panel_rows = from_root(features, "row", section_idx).reshape(
            feat_dev, row_blocks, block_size
        )
        picked = panel_rows[:, block_cols[:, section_idx, :]]
        total = total + jnp.einsum(
            "fbkj,bkij->fbi", picked, masked[:, section_idx], preferred_element_type=jnp.float32
        )
    aggregated = total.reshape(feat_dev, slab_rows).astype(jnp.bfloat16)
    agg_full = lax.all_gather(aggregated, "col", axis=0, tiled=True)
    preact = jnp.dot(weight, agg_full, preferred_element_type=jnp.float32)
    output = jax.nn.silu(preact).astype(jnp.bfloat16)
    sigmoid_pre = jax.nn.sigmoid(preact)
    dpre = (
        cotangent.astype(jnp.float32) * sigmoid_pre * (1.0 + preact * (1.0 - sigmoid_pre))
    ).astype(jnp.bfloat16)
    local_grad = lax.dot_general(
        dpre, agg_full, (((1,), (1,)), ((), ())), preferred_element_type=jnp.float32
    )
    grad_weight = lax.psum(local_grad, "row") / jnp.sqrt(jnp.float32(node_total))
    dpre_full, weight_full = (
        lax.all_gather(dpre, "col", axis=0, tiled=True),
        lax.all_gather(weight, "col", axis=0, tiled=True),
    )
    first_col = lax.axis_index("col") * feat_dev
    weight_cols = lax.dynamic_slice_in_dim(weight_full, first_col, feat_dev, 1)
    dagg = lax.dot_general(
        weight_cols, dpre_full, (((0,), (0,)), ((), ())), preferred_element_type=jnp.float32
    ).astype(jnp.bfloat16)
    contrib = jnp.einsum(
        "fbi,bskij->fbskj",
        dagg.reshape(feat_dev, local_blocks, block_size),
        masked,
        preferred_element_type=jnp.float32,
    )
    terms = (
        jnp.zeros((feat_dev, section_count * row_blocks, block_size), jnp.float32)
        .at[:, global_index]
        .add(contrib)
    )
    terms = terms.reshape(feat_dev, section_count * slab_rows)
    grad_features = lax.psum_scatter(terms, "row", scatter_dimension=1, tiled=True).astype(
        jnp.bfloat16
    )
    return (output, grad_weight, grad_features)


NT = (((1,), (1,)), ((), ()))


def link_table(block_cols, block_counts, row_blocks):
    blocks, sections, slots = block_cols.shape
    entries = blocks * slots
    dest = jnp.transpose(block_cols, (1, 0, 2)).reshape(sections, entries)
    ids = jnp.arange(entries, dtype=jnp.int32)
    span = jnp.arange(row_blocks, dtype=jnp.int32)
    keys = jnp.concatenate(
        [dest, jnp.broadcast_to(span[None], (sections, row_blocks))], axis=1
    )
    bound = jnp.concatenate([ids, jnp.full((row_blocks,), entries, jnp.int32)])
    hit = (dest[:, None, :] == keys[:, :, None]) & (ids[None, None, :] < bound[None, :, None])
    links = jnp.max(jnp.where(hit, ids[None, None, :] + 1, 0), axis=2)
    return jnp.concatenate(
        [block_cols.reshape(-1), block_counts.reshape(-1), links.reshape(-1)]
    )


def kernel(
    cols_n, scale,
    meta, feat, a, w, cot,
    out, gw, gf,
    av, fv, fb, acc, sagg, aggf, wf, wt, cotf, dpre, sout, sdag, rdag,
    gpart, grecv, gsend, gin, grow, ghalf, chain, tsend, trecv,
    loc, cot_s, cot_r, w_s, w_r, wf_s, wf_r, agg_s, agg_r, out_s, out_r,
    dag_s, dag_r, gw_s, gw_r, pair_s, pair_r,
):
    me = lax.axis_index("col")
    r = lax.axis_index("row")
    o = 1 - r
    fd, n = feat.shape
    nb, sections, slots, bs, _ = a.shape
    full = wf.shape[0]
    npd = n // cols_n
    bpd = npd // bs
    h = fd // 2
    entries = nb * slots
    table = nb * sections * slots
    links = table + nb * sections
    per = entries + nb
    chunk = math.gcd(full, 128)

    def peer(d):
        return lax.rem(me + d, cols_n)

    def source(d):
        return lax.rem(me + cols_n - d, cols_n)

    def rows(c, size):
        return pl.ds(pl.multiple_of(c * size, size), size)

    def remote(src, dst, ss, rs, where):
        return pltpu.make_async_remote_copy(
            src_ref=src, dst_ref=dst, send_sem=ss, recv_sem=rs,
            device_id=where, device_id_type=MESH,
        )

    def each(fn):
        @pl.loop(1, cols_n)
        def _(d):
            fn(d)

    barrier = pltpu.get_barrier_semaphore()
    pl.semaphore_signal(barrier, inc=1, device_id={"row": o}, device_id_type=MESH)
    each(lambda d: pl.semaphore_signal(
        barrier, inc=1, device_id={"col": peer(d)}, device_id_type=MESH))

    own_feat = pltpu.make_async_copy(feat, fv.at[r], loc.at[0])
    own_a = pltpu.make_async_copy(a.at[:, r], av.at[:, r], loc.at[1])
    other_a = pltpu.make_async_copy(a.at[:, o], av.at[:, o], loc.at[2])
    own_w = pltpu.make_async_copy(w, wf.at[rows(me, fd)], loc.at[3])
    own_cot = pltpu.make_async_copy(cot.at[:, rows(me, npd)], cotf.at[rows(me, fd)], loc.at[4])
    own_feat.start()
    own_a.start()
    other_a.start()
    own_w.start()
    own_cot.start()
    pl.semaphore_wait(barrier, cols_n)

    swap = remote(feat, fv.at[r], pair_s.at[0], pair_r.at[0], {"row": o})
    swap_in = remote(feat, fv.at[o], pair_s.at[0], pair_r.at[0], {"row": o})
    swap.start()

    def half_rows(c, half):
        return pl.ds(pl.multiple_of(c * fd + half * h, h), h)

    def w_copy(d, c):
        return remote(w.at[rows(r, h)], wf.at[half_rows(c, r)], w_s.at[d], w_r.at[d],
                      {"col": peer(d)})

    def cot_copy(d, c):
        return remote(cot.at[:, rows(peer(d), npd)], cotf.at[rows(c, fd)], cot_s.at[d],
                      cot_r.at[d], {"col": peer(d)})

    def wf_copy(d, half):
        part = wf.at[half_rows(source(d), half)]
        return remote(part, part, wf_s.at[d], wf_r.at[d], {"row": o})

    def agg_copy(d, c):
        return remote(sagg.at[peer(d)], aggf.at[rows(c, fd)], agg_s.at[d], agg_r.at[d],
                      {"col": peer(d)})

    def out_copy(d, c):
        return remote(sout.at[rows(peer(d), fd)], out.at[:, rows(c, npd)], out_s.at[d],
                      out_r.at[d], {"col": peer(d)})

    def dag_copy(d, c):
        return remote(sdag.at[rows(peer(d), fd)], rdag.at[:, rows(c, npd)], dag_s.at[d],
                      dag_r.at[d], {"col": peer(d)})

    def gw_copy(d, c):
        return remote(gsend.at[peer(d)], gin.at[c], gw_s.at[d], gw_r.at[d],
                      {"col": peer(d)})

    each(lambda d: w_copy(d, me).start())
    each(lambda d: cot_copy(d, me).start())

    def alive(count, k):
        return jnp.minimum(jnp.maximum(count - k, 0), 1).astype(f32)

    def split_blocks(s):
        for c in range(nb):
            fb[s, c] = fv[s, :, c * bs:(c + 1) * bs]

    def gathered(b, s):
        picks = []
        count = meta[table + b * sections + s]
        for k in range(slots):
            c = meta[b * (sections * slots) + s * slots + k]
            picks.append((fb[s, c].astype(f32) * alive(count, k)).astype(bf16))
        left = jnp.concatenate(picks, axis=1)
        right = jnp.concatenate([av[b, s, k] for k in range(slots)], axis=1)
        return lax.dot_general(left, right, NT, preferred_element_type=f32)

    own_feat.wait()
    split_blocks(r)
    own_a.wait()

    @pl.loop(0, nb, unroll=4)
    def _(b):
        acc[b] = gathered(b, r)

    swap_in.wait_recv()
    split_blocks(o)
    other_a.wait()

    def finish(c):
        parts = []
        for j in range(bpd):
            b = c * bpd + j
            parts.append((acc[b] + gathered(b, o)).astype(bf16))
        return jnp.concatenate(parts, axis=1)

    def send_agg(d):
        sagg[peer(d)] = finish(peer(d))
        agg_copy(d, me).start()

    each(send_agg)
    aggf[rows(me, fd), :] = finish(me)

    def forward_w(d):
        w_copy(d, source(d)).wait_recv()
        wf_copy(d, r).start()

    each(forward_w)
    own_w.wait()
    each(lambda d: wf_copy(d, o).wait_recv())
    for q in range(full // chunk):
        wt[:, pl.ds(q * chunk, chunk)] = wf[pl.ds(q * chunk, chunk), :].T
    own_cot.wait()
    each(lambda d: cot_copy(d, source(d)).wait_recv())
    each(lambda d: agg_copy(d, source(d)).wait_recv())

    for q in range(full // chunk):
        at = pl.ds(q * chunk, chunk)
        pre = jnp.dot(wf[at, :], aggf[...], preferred_element_type=f32)
        sig = jax.nn.sigmoid(pre)
        sout[at, :] = (pre * sig).astype(bf16)
        dpre[at, :] = (cotf[at, :].astype(f32) * sig * (1.0 + pre * (1.0 - sig))).astype(bf16)
    for q in range(full // chunk):
        at = pl.ds(q * chunk, chunk)
        sdag[at, :] = jnp.dot(wt[at, :], dpre[...], preferred_element_type=f32).astype(bf16)

    each(lambda d: dag_copy(d, me).start())
    each(lambda d: out_copy(d, me).start())
    rdag[:, rows(me, npd)] = sdag[rows(me, fd), :]
    own_out = pltpu.make_async_copy(sout.at[rows(me, fd)], out.at[:, rows(me, npd)], loc.at[5])
    own_out.start()

    per_chunk = chunk // fd
    for q in range(full // chunk):
        part = lax.dot_general(dpre[pl.ds(q * chunk, chunk), :], aggf[...], NT,
                               preferred_element_type=f32) * scale
        gpart[pl.ds(q * per_chunk, per_chunk)] = part.reshape(per_chunk, 2, h, full)
    gswap = remote(gpart.at[:, o], grecv, pair_s.at[1], pair_r.at[1], {"row": o})
    gswap.start()
    gswap.wait_recv()

    @pl.loop(0, cols_n)
    def _(c):
        gsend[c] = (gpart[c, r] + grecv[c]).astype(bf16)

    gin[me] = gsend[me]
    each(lambda d: gw_copy(d, me).start())

    each(lambda d: dag_copy(d, source(d)).wait_recv())
    chain[0] = jnp.zeros(chain.shape[1:], f32)

    def section(s):
        @pl.loop(0, nb, unroll=2)
        def _(b):
            count = meta[table + b * sections + s]
            right = jnp.concatenate([av[b, s, k] for k in range(slots)], axis=1)
            terms = jnp.dot(rdag[:, pl.ds(pl.multiple_of(b * bs, bs), bs)], right,
                            preferred_element_type=f32)
            for k in range(slots):
                e = b * slots + k
                live = alive(count, k)
                before = chain[meta[links + s * per + e]]
                chain[e + 1] = before + terms[:, k * bs:(k + 1) * bs] * live

    section(o)

    @pl.loop(0, nb, unroll=4)
    def _(c):
        tsend[c] = chain[meta[links + o * per + entries + c]]

    tswap = remote(tsend, trecv, pair_s.at[2], pair_r.at[2], {"row": o})
    tswap.start()
    section(r)
    tswap.wait_recv()

    @pl.loop(0, nb, unroll=4)
    def _(c):
        last = chain[meta[links + r * per + entries + c]]
        gf[:, pl.ds(pl.multiple_of(c * bs, bs), bs)] = (last + trecv[c]).astype(bf16)

    each(lambda d: gw_copy(d, source(d)).wait_recv())
    total = jnp.zeros((h, full), f32)
    for c in range(cols_n):
        total = total + gin[c].astype(f32)
    ghalf[...] = total
    gw[rows(r, h), :] = total
    rswap = remote(ghalf, grow, pair_s.at[3], pair_r.at[3], {"row": o})
    rswap.start()
    rswap.wait_recv()
    gw[rows(o, h), :] = grow[...]

    each(lambda d: out_copy(d, source(d)).wait_recv())
    own_out.wait()

    def drain(d):
        w_copy(d, me).wait_send()
        cot_copy(d, me).wait_send()
        wf_copy(d, r).wait_send()
        agg_copy(d, me).wait_send()
        dag_copy(d, me).wait_send()
        out_copy(d, me).wait_send()
        gw_copy(d, me).wait_send()

    each(drain)
    swap.wait_send()
    gswap.wait_send()
    tswap.wait_send()
    rswap.wait_send()


def fused(cols_n, features, a_blocks, block_cols, block_counts, weight, cotangent):
    fd, n = features.shape
    nb, sections, slots, bs, _ = a_blocks.shape
    full = weight.shape[1]
    npd = n // cols_n
    h = fd // 2
    scale = 1.0 / math.sqrt(n * sections)
    meta = link_table(block_cols, block_counts, n // bs)
    hbm = pl.BlockSpec(memory_space=pl.ANY)
    vmem = pl.BlockSpec(memory_space=pltpu.VMEM)
    dma = pltpu.SemaphoreType.DMA
    flops = 2 * fd * n * bs * sections * slots * 2 + 6 * full * full * npd
    return pl.pallas_call(
        functools.partial(kernel, cols_n, scale),
        out_shape=(
            jax.ShapeDtypeStruct((fd, n), bf16),
            jax.ShapeDtypeStruct((fd, full), f32),
            jax.ShapeDtypeStruct((fd, n), bf16),
        ),
        in_specs=[pl.BlockSpec(memory_space=pltpu.SMEM)] + [hbm] * 4,
        out_specs=(hbm, vmem, vmem),
        scratch_shapes=[
            pltpu.VMEM(a_blocks.shape, bf16),
            pltpu.VMEM((2, fd, n), bf16),
            pltpu.VMEM((2, n // bs, fd, bs), bf16),
            pltpu.VMEM((nb, fd, bs), f32),
            pltpu.VMEM((cols_n, fd, npd), bf16),
            pltpu.VMEM((full, npd), bf16),
            pltpu.VMEM((full, full), bf16),
            pltpu.VMEM((full, full), bf16),
            pltpu.VMEM((full, npd), bf16),
            pltpu.VMEM((full, npd), bf16),
            pltpu.VMEM((full, npd), bf16),
            pltpu.VMEM((full, npd), bf16),
            pltpu.VMEM((fd, n), bf16),
            pltpu.VMEM((cols_n, 2, h, full), f32),
            pltpu.VMEM((cols_n, h, full), f32),
            pltpu.VMEM((cols_n, h, full), bf16),
            pltpu.VMEM((cols_n, h, full), bf16),
            pltpu.VMEM((h, full), f32),
            pltpu.VMEM((h, full), f32),
            pltpu.VMEM((nb * slots + 1, fd, bs), f32),
            pltpu.VMEM((nb, fd, bs), f32),
            pltpu.VMEM((nb, fd, bs), f32),
            dma((6,)),
        ] + [dma((cols_n,))] * 14 + [dma((4,))] * 2,
        compiler_params=pltpu.CompilerParams(
            collective_id=0, has_side_effects=True, vmem_limit_bytes=40 * 2**20
        ),
        cost_estimate=pl.CostEstimate(
            flops=flops, bytes_accessed=a_blocks.size * 2 + 8 * fd * n,
            transcendentals=full * npd,
        ),
    )(meta, features, a_blocks, weight, cotangent)


def local(rows_n, cols_n, features, a_blocks, block_cols, block_counts, weight, cotangent):
    fd, n = features.shape
    bs = a_blocks.shape[-1]
    args = (features, a_blocks, block_cols, block_counts, weight, cotangent)
    fits = (
        rows_n == 2
        and a_blocks.shape[1] == 2
        and a_blocks.shape[0] * bs == n
        and bs % 128 == 0
        and n % (cols_n * bs) == 0
        and fd % 32 == 0
        and 128 % fd == 0
        and weight.shape[1] % 128 == 0
        and weight.shape[1] == fd * cols_n
    )
    return fused(cols_n, *args) if fits else plain(*args)


def solution(mesh):
    placed = (
        P("col", "row"),
        P("row", None, None, None, None),
        P("row", None, None),
        P("row", None),
        P("col", None),
        P("col", "row"),
    )
    return jax.shard_map(
        functools.partial(local, mesh.shape["row"], mesh.shape["col"]),
        mesh=mesh,
        in_specs=placed,
        out_specs=(P("col", "row"), P("col", None), P("col", "row")),
        check_vma=False,
    )
```

```python
import functools
import math

import jax
import jax.numpy as jnp
from jax import lax
from jax.experimental import pallas as pl
from jax.experimental.pallas import tpu as pltpu
from jax.sharding import PartitionSpec as P

MESH = pl.DeviceIdType.MESH
f32 = jnp.float32
bf16 = jnp.bfloat16


def from_root(value, axis, source):
    kept = jnp.where(lax.axis_index(axis) == source, value, 0).astype(value.dtype)
    return lax.psum(kept, axis)


def plain(features, a_blocks, block_cols, block_counts, weight, cotangent):
    feat_dev = features.shape[0]
    slab_rows = features.shape[1]
    block_size = a_blocks.shape[-1]
    local_blocks = a_blocks.shape[0]
    section_count = a_blocks.shape[1]
    slot_count = a_blocks.shape[2]
    row_blocks = slab_rows // block_size
    slot_ids = jnp.arange(slot_count, dtype=jnp.int32)
    live_mask = (slot_ids[None, None, :] < block_counts[:, :, None]).astype(jnp.bfloat16)
    masked = a_blocks * live_mask[:, :, :, None, None]
    global_index = (
        jnp.arange(section_count, dtype=jnp.int32)[None, :, None] * row_blocks + block_cols
    )
    node_total = slab_rows * lax.axis_size("row")
    total = jnp.zeros((feat_dev, local_blocks, block_size), jnp.float32)
    for section_idx in range(lax.axis_size("row")):
        panel_rows = from_root(features, "row", section_idx).reshape(
            feat_dev, row_blocks, block_size
        )
        picked = panel_rows[:, block_cols[:, section_idx, :]]
        total = total + jnp.einsum(
            "fbkj,bkij->fbi", picked, masked[:, section_idx], preferred_element_type=jnp.float32
        )
    aggregated = total.reshape(feat_dev, slab_rows).astype(jnp.bfloat16)
    agg_full = lax.all_gather(aggregated, "col", axis=0, tiled=True)
    preact = jnp.dot(weight, agg_full, preferred_element_type=jnp.float32)
    output = jax.nn.silu(preact).astype(jnp.bfloat16)
    sigmoid_pre = jax.nn.sigmoid(preact)
    dpre = (
        cotangent.astype(jnp.float32) * sigmoid_pre * (1.0 + preact * (1.0 - sigmoid_pre))
    ).astype(jnp.bfloat16)
    local_grad = lax.dot_general(
        dpre, agg_full, (((1,), (1,)), ((), ())), preferred_element_type=jnp.float32
    )
    grad_weight = lax.psum(local_grad, "row") / jnp.sqrt(jnp.float32(node_total))
    dpre_full, weight_full = (
        lax.all_gather(dpre, "col", axis=0, tiled=True),
        lax.all_gather(weight, "col", axis=0, tiled=True),
    )
    first_col = lax.axis_index("col") * feat_dev
    weight_cols = lax.dynamic_slice_in_dim(weight_full, first_col, feat_dev, 1)
    dagg = lax.dot_general(
        weight_cols, dpre_full, (((0,), (0,)), ((), ())), preferred_element_type=jnp.float32
    ).astype(jnp.bfloat16)
    contrib = jnp.einsum(
        "fbi,bskij->fbskj",
        dagg.reshape(feat_dev, local_blocks, block_size),
        masked,
        preferred_element_type=jnp.float32,
    )
    terms = (
        jnp.zeros((feat_dev, section_count * row_blocks, block_size), jnp.float32)
        .at[:, global_index]
        .add(contrib)
    )
    terms = terms.reshape(feat_dev, section_count * slab_rows)
    grad_features = lax.psum_scatter(terms, "row", scatter_dimension=1, tiled=True).astype(
        jnp.bfloat16
    )
    return (output, grad_weight, grad_features)


NT = (((1,), (1,)), ((), ()))


def link_rows(block_cols, s, nb, slots):
    entries = nb * slots
    lane = lax.broadcasted_iota(jnp.int32, (1, 128), 1)
    dest = jnp.full((1, 128), -1, jnp.int32)
    for e in range(entries):
        dest = jnp.where(lane == e, block_cols[s, e % slots, e // slots], dest)
    across = jnp.broadcast_to(dest, (128, 128))
    down = across.T
    first = lax.broadcasted_iota(jnp.int32, (128, 128), 0)
    second = lax.broadcasted_iota(jnp.int32, (128, 128), 1)
    before = jnp.where((down == across) & (first < second), first + 1, 0)
    last = jnp.where(down == second, first + 1, 0)
    return jnp.max(before, axis=0, keepdims=True), jnp.max(last, axis=0, keepdims=True)


def kernel(
    cols_n, scale,
    block_cols, counts, feat, a, w, cot,
    out, gw, gf,
    av, fv, fb, acc, sagg, aggf, wf, wt, cotf, dpre, sout, sdag, rdag,
    gpart, grecv, gsend, gin, grow, ghalf, chain, tsend, trecv, table_v, table,
    loc, cot_s, cot_r, w_s, w_r, wf_s, wf_r, agg_s, agg_r, out_s, out_r,
    dag_s, dag_r, gw_s, gw_r, pair_s, pair_r,
):
    me = lax.axis_index("col")
    r = lax.axis_index("row")
    o = 1 - r
    fd, n = feat.shape
    nb, sections, slots, bs, _ = a.shape
    full = wf.shape[0]
    npd = n // cols_n
    bpd = npd // bs
    h = fd // 2
    entries = nb * slots
    chunk = math.gcd(full, 128)

    def peer(d):
        return lax.rem(me + d, cols_n)

    def source(d):
        return lax.rem(me + cols_n - d, cols_n)

    def rows(c, size):
        return pl.ds(pl.multiple_of(c * size, size), size)

    def remote(src, dst, ss, rs, where):
        return pltpu.make_async_remote_copy(
            src_ref=src, dst_ref=dst, send_sem=ss, recv_sem=rs,
            device_id=where, device_id_type=MESH,
        )

    def each(fn):
        @pl.loop(1, cols_n)
        def _(d):
            fn(d)

    barrier = pltpu.get_barrier_semaphore()
    pl.semaphore_signal(barrier, inc=1, device_id={"row": o}, device_id_type=MESH)
    each(lambda d: pl.semaphore_signal(
        barrier, inc=1, device_id={"col": peer(d)}, device_id_type=MESH))

    own_feat = pltpu.make_async_copy(feat, fv.at[r], loc.at[0])
    own_a = pltpu.make_async_copy(a.at[:, r], av.at[:, r], loc.at[1])
    other_a = pltpu.make_async_copy(a.at[:, o], av.at[:, o], loc.at[2])
    own_w = pltpu.make_async_copy(w, wf.at[rows(me, fd)], loc.at[3])
    own_cot = pltpu.make_async_copy(cot.at[:, rows(me, npd)], cotf.at[rows(me, fd)], loc.at[4])
    own_feat.start()
    own_a.start()
    other_a.start()
    own_w.start()
    own_cot.start()
    pl.semaphore_wait(barrier, cols_n)

    swap = remote(feat, fv.at[r], pair_s.at[0], pair_r.at[0], {"row": o})
    swap_in = remote(feat, fv.at[o], pair_s.at[0], pair_r.at[0], {"row": o})
    swap.start()

    def half_rows(c, half):
        return pl.ds(pl.multiple_of(c * fd + half * h, h), h)

    def w_copy(d, c):
        return remote(w.at[rows(r, h)], wf.at[half_rows(c, r)], w_s.at[d], w_r.at[d],
                      {"col": peer(d)})

    def cot_copy(d, c):
        return remote(cot.at[:, rows(peer(d), npd)], cotf.at[rows(c, fd)], cot_s.at[d],
                      cot_r.at[d], {"col": peer(d)})

    def wf_copy(d, half):
        part = wf.at[half_rows(source(d), half)]
        return remote(part, part, wf_s.at[d], wf_r.at[d], {"row": o})

    def agg_copy(d, c):
        return remote(sagg.at[peer(d)], aggf.at[rows(c, fd)], agg_s.at[d], agg_r.at[d],
                      {"col": peer(d)})

    def out_copy(d, c):
        return remote(sout.at[rows(peer(d), fd)], out.at[:, rows(c, npd)], out_s.at[d],
                      out_r.at[d], {"col": peer(d)})

    def dag_copy(d, c):
        return remote(sdag.at[rows(peer(d), fd)], rdag.at[:, rows(c, npd)], dag_s.at[d],
                      dag_r.at[d], {"col": peer(d)})

    def gw_copy(d, c):
        return remote(gsend.at[peer(d)], gin.at[c], gw_s.at[d], gw_r.at[d],
                      {"col": peer(d)})

    each(lambda d: w_copy(d, me).start())
    each(lambda d: cot_copy(d, me).start())

    def alive(count, k):
        return jnp.minimum(jnp.maximum(count - k, 0), 1).astype(f32)

    def split_blocks(s):
        for c in range(nb):
            fb[s, c] = fv[s, :, c * bs:(c + 1) * bs]

    def gathered(b, s):
        picks = []
        count = counts[s, b]
        for k in range(slots):
            c = block_cols[s, k, b]
            picks.append((fb[s, c].astype(f32) * alive(count, k)).astype(bf16))
        left = jnp.concatenate(picks, axis=1)
        right = jnp.concatenate([av[b, s, k] for k in range(slots)], axis=1)
        return lax.dot_general(left, right, NT, preferred_element_type=f32)

    own_feat.wait()
    split_blocks(r)
    own_a.wait()

    @pl.loop(0, nb, unroll=4)
    def _(b):
        acc[b] = gathered(b, r)

    swap_in.wait_recv()
    split_blocks(o)
    other_a.wait()

    def finish(c):
        parts = []
        for j in range(bpd):
            b = c * bpd + j
            parts.append((acc[b] + gathered(b, o)).astype(bf16))
        return jnp.concatenate(parts, axis=1)

    def send_agg(d):
        sagg[peer(d)] = finish(peer(d))
        agg_copy(d, me).start()

    each(send_agg)
    aggf[rows(me, fd), :] = finish(me)

    def forward_w(d):
        w_copy(d, source(d)).wait_recv()
        wf_copy(d, r).start()

    each(forward_w)
    for s in range(sections):
        by_entry, by_block = link_rows(block_cols, s, nb, slots)
        table_v[2 * s:2 * s + 1, :] = by_entry
        table_v[2 * s + 1:2 * s + 2, :] = by_block
    put_table = pltpu.make_async_copy(table_v, table, loc.at[6])
    put_table.start()
    own_w.wait()
    each(lambda d: wf_copy(d, o).wait_recv())
    for q in range(full // chunk):
        wt[:, pl.ds(q * chunk, chunk)] = wf[pl.ds(q * chunk, chunk), :].T
    own_cot.wait()
    each(lambda d: cot_copy(d, source(d)).wait_recv())
    each(lambda d: agg_copy(d, source(d)).wait_recv())

    for q in range(full // chunk):
        at = pl.ds(q * chunk, chunk)
        pre = jnp.dot(wf[at, :], aggf[...], preferred_element_type=f32)
        sig = jax.nn.sigmoid(pre)
        sout[at, :] = (pre * sig).astype(bf16)
        dpre[at, :] = (cotf[at, :].astype(f32) * sig * (1.0 + pre * (1.0 - sig))).astype(bf16)
    for q in range(full // chunk):
        at = pl.ds(q * chunk, chunk)
        sdag[at, :] = jnp.dot(wt[at, :], dpre[...], preferred_element_type=f32).astype(bf16)

    each(lambda d: dag_copy(d, me).start())
    each(lambda d: out_copy(d, me).start())
    rdag[:, rows(me, npd)] = sdag[rows(me, fd), :]
    own_out = pltpu.make_async_copy(sout.at[rows(me, fd)], out.at[:, rows(me, npd)], loc.at[5])
    own_out.start()

    per_chunk = chunk // fd
    for q in range(full // chunk):
        part = lax.dot_general(dpre[pl.ds(q * chunk, chunk), :], aggf[...], NT,
                               preferred_element_type=f32) * scale
        gpart[pl.ds(q * per_chunk, per_chunk)] = part.reshape(per_chunk, 2, h, full)
    gswap = remote(gpart.at[:, o], grecv, pair_s.at[1], pair_r.at[1], {"row": o})
    gswap.start()
    gswap.wait_recv()

    @pl.loop(0, cols_n)
    def _(c):
        gsend[c] = (gpart[c, r] + grecv[c]).astype(bf16)

    gin[me] = gsend[me]
    each(lambda d: gw_copy(d, me).start())

    put_table.wait()
    each(lambda d: dag_copy(d, source(d)).wait_recv())
    chain[0] = jnp.zeros(chain.shape[1:], f32)

    def section(s):
        @pl.loop(0, nb, unroll=2)
        def _(b):
            count = counts[s, b]
            right = jnp.concatenate([av[b, s, k] for k in range(slots)], axis=1)
            terms = jnp.dot(rdag[:, pl.ds(pl.multiple_of(b * bs, bs), bs)], right,
                            preferred_element_type=f32)
            for k in range(slots):
                e = b * slots + k
                live = alive(count, k)
                before = chain[table[2 * s, e]]
                chain[e + 1] = before + terms[:, k * bs:(k + 1) * bs] * live

    section(o)

    @pl.loop(0, nb, unroll=4)
    def _(c):
        tsend[c] = chain[table[2 * o + 1, c]]

    tswap = remote(tsend, trecv, pair_s.at[2], pair_r.at[2], {"row": o})
    tswap.start()
    section(r)
    tswap.wait_recv()

    @pl.loop(0, nb, unroll=4)
    def _(c):
        last = chain[table[2 * r + 1, c]]
        gf[:, pl.ds(pl.multiple_of(c * bs, bs), bs)] = (last + trecv[c]).astype(bf16)

    each(lambda d: gw_copy(d, source(d)).wait_recv())
    total = jnp.zeros((h, full), f32)
    for c in range(cols_n):
        total = total + gin[c].astype(f32)
    ghalf[...] = total
    gw[rows(r, h), :] = total
    rswap = remote(ghalf, grow, pair_s.at[3], pair_r.at[3], {"row": o})
    rswap.start()
    rswap.wait_recv()
    gw[rows(o, h), :] = grow[...]

    each(lambda d: out_copy(d, source(d)).wait_recv())
    own_out.wait()

    def drain(d):
        w_copy(d, me).wait_send()
        cot_copy(d, me).wait_send()
        wf_copy(d, r).wait_send()
        agg_copy(d, me).wait_send()
        dag_copy(d, me).wait_send()
        out_copy(d, me).wait_send()
        gw_copy(d, me).wait_send()

    each(drain)
    swap.wait_send()
    gswap.wait_send()
    tswap.wait_send()
    rswap.wait_send()


def fused(cols_n, features, a_blocks, block_cols, block_counts, weight, cotangent):
    fd, n = features.shape
    nb, sections, slots, bs, _ = a_blocks.shape
    full = weight.shape[1]
    npd = n // cols_n
    h = fd // 2
    scale = 1.0 / math.sqrt(n * sections)
    hbm = pl.BlockSpec(memory_space=pl.ANY)
    vmem = pl.BlockSpec(memory_space=pltpu.VMEM)
    dma = pltpu.SemaphoreType.DMA
    flops = 2 * fd * n * bs * sections * slots * 2 + 6 * full * full * npd
    return pl.pallas_call(
        functools.partial(kernel, cols_n, scale),
        out_shape=(
            jax.ShapeDtypeStruct((fd, n), bf16),
            jax.ShapeDtypeStruct((fd, full), f32),
            jax.ShapeDtypeStruct((fd, n), bf16),
        ),
        in_specs=[pl.BlockSpec(memory_space=pltpu.SMEM)] * 2 + [hbm] * 4,
        out_specs=(hbm, vmem, vmem),
        scratch_shapes=[
            pltpu.VMEM(a_blocks.shape, bf16),
            pltpu.VMEM((2, fd, n), bf16),
            pltpu.VMEM((2, n // bs, fd, bs), bf16),
            pltpu.VMEM((nb, fd, bs), f32),
            pltpu.VMEM((cols_n, fd, npd), bf16),
            pltpu.VMEM((full, npd), bf16),
            pltpu.VMEM((full, full), bf16),
            pltpu.VMEM((full, full), bf16),
            pltpu.VMEM((full, npd), bf16),
            pltpu.VMEM((full, npd), bf16),
            pltpu.VMEM((full, npd), bf16),
            pltpu.VMEM((full, npd), bf16),
            pltpu.VMEM((fd, n), bf16),
            pltpu.VMEM((cols_n, 2, h, full), f32),
            pltpu.VMEM((cols_n, h, full), f32),
            pltpu.VMEM((cols_n, h, full), bf16),
            pltpu.VMEM((cols_n, h, full), bf16),
            pltpu.VMEM((h, full), f32),
            pltpu.VMEM((h, full), f32),
            pltpu.VMEM((nb * slots + 1, fd, bs), f32),
            pltpu.VMEM((nb, fd, bs), f32),
            pltpu.VMEM((nb, fd, bs), f32),
            pltpu.VMEM((8, 128), jnp.int32),
            pltpu.SMEM((8, 128), jnp.int32),
            dma((7,)),
        ] + [dma((cols_n,))] * 14 + [dma((4,))] * 2,
        compiler_params=pltpu.CompilerParams(
            collective_id=0, has_side_effects=True, vmem_limit_bytes=62 * 2**20
        ),
        cost_estimate=pl.CostEstimate(
            flops=flops, bytes_accessed=a_blocks.size * 2 + 8 * fd * n,
            transcendentals=full * npd,
        ),
    )(jnp.transpose(block_cols, (1, 2, 0)), block_counts.T, features, a_blocks, weight, cotangent)


def local(rows_n, cols_n, features, a_blocks, block_cols, block_counts, weight, cotangent):
    fd, n = features.shape
    bs = a_blocks.shape[-1]
    args = (features, a_blocks, block_cols, block_counts, weight, cotangent)
    fits = (
        rows_n == 2
        and a_blocks.shape[1] == 2
        and a_blocks.shape[0] * bs == n
        and bs % 128 == 0
        and n % (cols_n * bs) == 0
        and fd % 32 == 0
        and a_blocks.shape[0] * a_blocks.shape[2] <= 128
        and a_blocks.shape[0] <= 128
        and 128 % fd == 0
        and weight.shape[1] % 128 == 0
        and weight.shape[1] == fd * cols_n
    )
    return fused(cols_n, *args) if fits else plain(*args)


def solution(mesh):
    placed = (
        P("col", "row"),
        P("row", None, None, None, None),
        P("row", None, None),
        P("row", None),
        P("col", None),
        P("col", "row"),
    )
    return jax.shard_map(
        functools.partial(local, mesh.shape["row"], mesh.shape["col"]),
        mesh=mesh,
        in_specs=placed,
        out_specs=(P("col", "row"), P("col", None), P("col", "row")),
        check_vma=False,
    )
```

```python
import functools
import math

import jax
import jax.numpy as jnp
from jax import lax
from jax.experimental import pallas as pl
from jax.experimental.pallas import tpu as pltpu
from jax.sharding import PartitionSpec as P

MESH = pl.DeviceIdType.MESH
f32 = jnp.float32
bf16 = jnp.bfloat16


def from_root(value, axis, source):
    kept = jnp.where(lax.axis_index(axis) == source, value, 0).astype(value.dtype)
    return lax.psum(kept, axis)


def plain(features, a_blocks, block_cols, block_counts, weight, cotangent):
    feat_dev = features.shape[0]
    slab_rows = features.shape[1]
    block_size = a_blocks.shape[-1]
    local_blocks = a_blocks.shape[0]
    section_count = a_blocks.shape[1]
    slot_count = a_blocks.shape[2]
    row_blocks = slab_rows // block_size
    slot_ids = jnp.arange(slot_count, dtype=jnp.int32)
    live_mask = (slot_ids[None, None, :] < block_counts[:, :, None]).astype(jnp.bfloat16)
    masked = a_blocks * live_mask[:, :, :, None, None]
    global_index = (
        jnp.arange(section_count, dtype=jnp.int32)[None, :, None] * row_blocks + block_cols
    )
    node_total = slab_rows * lax.axis_size("row")
    total = jnp.zeros((feat_dev, local_blocks, block_size), jnp.float32)
    for section_idx in range(lax.axis_size("row")):
        panel_rows = from_root(features, "row", section_idx).reshape(
            feat_dev, row_blocks, block_size
        )
        picked = panel_rows[:, block_cols[:, section_idx, :]]
        total = total + jnp.einsum(
            "fbkj,bkij->fbi", picked, masked[:, section_idx], preferred_element_type=jnp.float32
        )
    aggregated = total.reshape(feat_dev, slab_rows).astype(jnp.bfloat16)
    agg_full = lax.all_gather(aggregated, "col", axis=0, tiled=True)
    preact = jnp.dot(weight, agg_full, preferred_element_type=jnp.float32)
    output = jax.nn.silu(preact).astype(jnp.bfloat16)
    sigmoid_pre = jax.nn.sigmoid(preact)
    dpre = (
        cotangent.astype(jnp.float32) * sigmoid_pre * (1.0 + preact * (1.0 - sigmoid_pre))
    ).astype(jnp.bfloat16)
    local_grad = lax.dot_general(
        dpre, agg_full, (((1,), (1,)), ((), ())), preferred_element_type=jnp.float32
    )
    grad_weight = lax.psum(local_grad, "row") / jnp.sqrt(jnp.float32(node_total))
    dpre_full, weight_full = (
        lax.all_gather(dpre, "col", axis=0, tiled=True),
        lax.all_gather(weight, "col", axis=0, tiled=True),
    )
    first_col = lax.axis_index("col") * feat_dev
    weight_cols = lax.dynamic_slice_in_dim(weight_full, first_col, feat_dev, 1)
    dagg = lax.dot_general(
        weight_cols, dpre_full, (((0,), (0,)), ((), ())), preferred_element_type=jnp.float32
    ).astype(jnp.bfloat16)
    contrib = jnp.einsum(
        "fbi,bskij->fbskj",
        dagg.reshape(feat_dev, local_blocks, block_size),
        masked,
        preferred_element_type=jnp.float32,
    )
    terms = (
        jnp.zeros((feat_dev, section_count * row_blocks, block_size), jnp.float32)
        .at[:, global_index]
        .add(contrib)
    )
    terms = terms.reshape(feat_dev, section_count * slab_rows)
    grad_features = lax.psum_scatter(terms, "row", scatter_dimension=1, tiled=True).astype(
        jnp.bfloat16
    )
    return (output, grad_weight, grad_features)


NT = (((1,), (1,)), ((), ()))


def link_rows(block_cols, s, nb, slots):
    entries = nb * slots
    lane = lax.broadcasted_iota(jnp.int32, (1, 128), 1)
    dest = jnp.full((1, 128), -1, jnp.int32)
    for e in range(entries):
        dest = jnp.where(lane == e, block_cols[s, e % slots, e // slots], dest)
    across = jnp.broadcast_to(dest, (128, 128))
    down = across.T
    first = lax.broadcasted_iota(jnp.int32, (128, 128), 0)
    second = lax.broadcasted_iota(jnp.int32, (128, 128), 1)
    before = jnp.where((down == across) & (first < second), first + 1, 0)
    last = jnp.where(down == second, first + 1, 0)
    return jnp.max(before, axis=0, keepdims=True), jnp.max(last, axis=0, keepdims=True)


def kernel(
    cols_n, scale,
    block_cols, counts, feat, a, w, cot,
    out, gw, gf,
    av, fv, fb, acc, sagg, aggf, wf, wt, cotf, dpre, sout, sdag, rdag,
    gpart, grecv, gsend, gnear, gsum, gmid, gfar, grow, ghalf, chain, tsend, trecv, table_v, table,
    loc, cot_s, cot_r, w_s, w_r, wf_s, wf_r, agg_s, agg_r, out_s, out_r,
    dag_s, dag_r, gw_s, gw_r, gn_s, gn_r, wn_s, wn_r, pair_s, pair_r,
):
    me = lax.axis_index("col")
    r = lax.axis_index("row")
    o = 1 - r
    fd, n = feat.shape
    nb, sections, slots, bs, _ = a.shape
    full = wf.shape[0]
    npd = n // cols_n
    bpd = npd // bs
    h = fd // 2
    entries = nb * slots
    chunk = math.gcd(full, 128)

    def peer(d):
        return lax.rem(me + d, cols_n)

    def source(d):
        return lax.rem(me + cols_n - d, cols_n)

    def rows(c, size):
        return pl.ds(pl.multiple_of(c * size, size), size)

    def remote(src, dst, ss, rs, where):
        return pltpu.make_async_remote_copy(
            src_ref=src, dst_ref=dst, send_sem=ss, recv_sem=rs,
            device_id=where, device_id_type=MESH,
        )

    def each(fn):
        @pl.loop(1, cols_n)
        def _(d):
            fn(d)

    barrier = pltpu.get_barrier_semaphore()
    pl.semaphore_signal(barrier, inc=1, device_id={"row": o}, device_id_type=MESH)
    each(lambda d: pl.semaphore_signal(
        barrier, inc=1, device_id={"col": peer(d)}, device_id_type=MESH))

    own_feat = pltpu.make_async_copy(feat, fv.at[r], loc.at[0])
    own_a = pltpu.make_async_copy(a.at[:, r], av.at[:, r], loc.at[1])
    other_a = pltpu.make_async_copy(a.at[:, o], av.at[:, o], loc.at[2])
    own_w = pltpu.make_async_copy(w, wf.at[rows(me, fd)], loc.at[3])
    own_cot = pltpu.make_async_copy(cot.at[:, rows(me, npd)], cotf.at[rows(me, fd)], loc.at[4])
    own_feat.start()
    own_a.start()
    other_a.start()
    own_w.start()
    own_cot.start()
    pl.semaphore_wait(barrier, cols_n)

    swap = remote(feat, fv.at[r], pair_s.at[0], pair_r.at[0], {"row": o})
    swap_in = remote(feat, fv.at[o], pair_s.at[0], pair_r.at[0], {"row": o})
    swap.start()

    def half_rows(c, half):
        return pl.ds(pl.multiple_of(c * fd + half * h, h), h)

    lo = math.gcd(cols_n, 4)
    hi = cols_n // lo
    my_lo = lax.rem(me, lo)
    my_hi = me // lo

    def near(v):
        return my_hi * lo + lax.rem(my_lo + v, lo)

    def far(u):
        return lax.rem(my_hi + u, hi) * lo + my_lo

    def origin(u, v):
        return lax.rem(my_hi + hi - u, hi) * lo + lax.rem(my_lo + lo - v, lo)

    def w_far(u, c):
        return remote(w.at[rows(r, h)], wf.at[half_rows(c, r)], w_s.at[u], w_r.at[u],
                      {"col": far(u)})

    def w_near(u, v, c):
        part = wf.at[half_rows(c, r)]
        return remote(part, part, wn_s.at[u, v], wn_r.at[u, v], {"col": near(v)})

    def cot_copy(d, c):
        return remote(cot.at[:, rows(peer(d), npd)], cotf.at[rows(c, fd)], cot_s.at[d],
                      cot_r.at[d], {"col": peer(d)})

    def wf_copy(d, half):
        part = wf.at[half_rows(origin(d // lo, lax.rem(d, lo)), half)]
        return remote(part, part, wf_s.at[d], wf_r.at[d], {"row": o})

    def agg_copy(d, c):
        return remote(sagg.at[peer(d)], aggf.at[rows(c, fd)], agg_s.at[d], agg_r.at[d],
                      {"col": peer(d)})

    def out_copy(d, c):
        return remote(sout.at[rows(peer(d), fd)], out.at[:, rows(c, npd)], out_s.at[d],
                      out_r.at[d], {"col": peer(d)})

    def dag_copy(d, c):
        return remote(sdag.at[rows(peer(d), fd)], rdag.at[:, rows(c, npd)], dag_s.at[d],
                      dag_r.at[d], {"col": peer(d)})

    def gw_near(v):
        return remote(gsend.at[:, lax.rem(my_lo + v, lo)], gnear.at[v], gn_s.at[v], gn_r.at[v],
                      {"col": near(v)})

    def gw_far(u):
        return remote(gmid.at[lax.rem(my_hi + u, hi)], gfar.at[u], gw_s.at[u], gw_r.at[u],
                      {"col": far(u)})

    for u in range(1, hi):
        w_far(u, me).start()
    own_w.wait()
    for v in range(1, lo):
        w_near(0, v, me).start()
    each(lambda d: cot_copy(d, me).start())

    def alive(count, k):
        return jnp.minimum(jnp.maximum(count - k, 0), 1).astype(f32)

    def split_blocks(s):
        for c in range(nb):
            fb[s, c] = fv[s, :, c * bs:(c + 1) * bs]

    def gathered(b, s):
        picks = []
        count = counts[s, b]
        for k in range(slots):
            c = block_cols[s, k, b]
            picks.append((fb[s, c].astype(f32) * alive(count, k)).astype(bf16))
        left = jnp.concatenate(picks, axis=1)
        right = jnp.concatenate([av[b, s, k] for k in range(slots)], axis=1)
        return lax.dot_general(left, right, NT, preferred_element_type=f32)

    own_feat.wait()
    split_blocks(r)
    own_a.wait()

    @pl.loop(0, nb, unroll=4)
    def _(b):
        acc[b] = gathered(b, r)

    for u in range(1, hi):
        w_far(u, origin(u, 0)).wait_recv()
        for v in range(1, lo):
            w_near(u, v, origin(u, 0)).start()

    swap_in.wait_recv()
    split_blocks(o)
    other_a.wait()

    def finish(c):
        parts = []
        for j in range(bpd):
            b = c * bpd + j
            parts.append((acc[b] + gathered(b, o)).astype(bf16))
        return jnp.concatenate(parts, axis=1)

    def send_agg(d):
        sagg[peer(d)] = finish(peer(d))
        agg_copy(d, me).start()

    each(send_agg)
    aggf[rows(me, fd), :] = finish(me)

    for d in range(1, cols_n):
        u, v = d // lo, d % lo
        if v:
            w_near(u, v, origin(u, v)).wait_recv()
        wf_copy(d, r).start()
    for s in range(sections):
        by_entry, by_block = link_rows(block_cols, s, nb, slots)
        table_v[2 * s:2 * s + 1, :] = by_entry
        table_v[2 * s + 1:2 * s + 2, :] = by_block
    put_table = pltpu.make_async_copy(table_v, table, loc.at[6])
    put_table.start()
    each(lambda d: wf_copy(d, o).wait_recv())
    for q in range(full // chunk):
        wt[:, pl.ds(q * chunk, chunk)] = wf[pl.ds(q * chunk, chunk), :].T
    own_cot.wait()
    each(lambda d: cot_copy(d, source(d)).wait_recv())
    each(lambda d: agg_copy(d, source(d)).wait_recv())

    for q in range(full // chunk):
        at = pl.ds(q * chunk, chunk)
        pre = jnp.dot(wf[at, :], aggf[...], preferred_element_type=f32)
        sig = jax.nn.sigmoid(pre)
        sout[at, :] = (pre * sig).astype(bf16)
        dpre[at, :] = (cotf[at, :].astype(f32) * sig * (1.0 + pre * (1.0 - sig))).astype(bf16)
    for q in range(full // chunk):
        at = pl.ds(q * chunk, chunk)
        sdag[at, :] = jnp.dot(wt[at, :], dpre[...], preferred_element_type=f32).astype(bf16)

    each(lambda d: dag_copy(d, me).start())
    rdag[:, rows(me, npd)] = sdag[rows(me, fd), :]
    own_out = pltpu.make_async_copy(sout.at[rows(me, fd)], out.at[:, rows(me, npd)], loc.at[5])
    own_out.start()

    per_chunk = chunk // fd
    for q in range(full // chunk):
        part = lax.dot_general(dpre[pl.ds(q * chunk, chunk), :], aggf[...], NT,
                               preferred_element_type=f32) * scale
        gpart[pl.ds(q * per_chunk, per_chunk)] = part.reshape(per_chunk, 2, h, full)
    gswap = remote(gpart.at[:, o], grecv, pair_s.at[1], pair_r.at[1], {"row": o})
    gswap.start()
    gswap.wait_recv()

    @pl.loop(0, cols_n)
    def _(c):
        both = gpart[c, r] + grecv[c]
        grecv[c] = both
        gsend[c // lo, lax.rem(c, lo)] = both.astype(bf16)

    for v in range(1, lo):
        gw_near(v).start()
    each(lambda d: out_copy(d, me).start())

    put_table.wait()
    each(lambda d: dag_copy(d, source(d)).wait_recv())
    chain[0] = jnp.zeros(chain.shape[1:], f32)

    def section(s):
        @pl.loop(0, nb, unroll=2)
        def _(b):
            count = counts[s, b]
            right = jnp.concatenate([av[b, s, k] for k in range(slots)], axis=1)
            terms = jnp.dot(rdag[:, pl.ds(pl.multiple_of(b * bs, bs), bs)], right,
                            preferred_element_type=f32)
            for k in range(slots):
                e = b * slots + k
                live = alive(count, k)
                before = chain[table[2 * s, e]]
                chain[e + 1] = before + terms[:, k * bs:(k + 1) * bs] * live

    section(o)

    @pl.loop(0, nb, unroll=4)
    def _(c):
        tsend[c] = chain[table[2 * o + 1, c]]

    tswap = remote(tsend, trecv, pair_s.at[2], pair_r.at[2], {"row": o})
    tswap.start()
    for v in range(1, lo):
        gw_near(v).wait_recv()
    for u in range(hi):
        level = grecv[u * lo + my_lo]
        for v in range(1, lo):
            level = level + gnear[v, u].astype(f32)
        gsum[u] = level
        gmid[u] = level.astype(bf16)
    for u in range(1, hi):
        gw_far(u).start()
    section(r)
    tswap.wait_recv()

    @pl.loop(0, nb, unroll=4)
    def _(c):
        last = chain[table[2 * r + 1, c]]
        gf[:, pl.ds(pl.multiple_of(c * bs, bs), bs)] = (last + trecv[c]).astype(bf16)

    total = gsum[my_hi]
    for u in range(1, hi):
        gw_far(u).wait_recv()
        total = total + gfar[u].astype(f32)
    ghalf[...] = total
    gw[rows(r, h), :] = total
    rswap = remote(ghalf, grow, pair_s.at[3], pair_r.at[3], {"row": o})
    rswap.start()
    rswap.wait_recv()
    gw[rows(o, h), :] = grow[...]

    each(lambda d: out_copy(d, source(d)).wait_recv())
    own_out.wait()

    def drain(d):
        cot_copy(d, me).wait_send()
        wf_copy(d, r).wait_send()
        agg_copy(d, me).wait_send()
        dag_copy(d, me).wait_send()
        out_copy(d, me).wait_send()

    each(drain)
    for u in range(hi):
        for v in range(1, lo):
            w_near(u, v, origin(u, 0)).wait_send()
    for u in range(1, hi):
        w_far(u, me).wait_send()
        gw_far(u).wait_send()
    for v in range(1, lo):
        gw_near(v).wait_send()
    swap.wait_send()
    gswap.wait_send()
    tswap.wait_send()
    rswap.wait_send()


def fused(cols_n, features, a_blocks, block_cols, block_counts, weight, cotangent):
    fd, n = features.shape
    nb, sections, slots, bs, _ = a_blocks.shape
    full = weight.shape[1]
    npd = n // cols_n
    h = fd // 2
    lo = math.gcd(cols_n, 4)
    hi = cols_n // lo
    scale = 1.0 / math.sqrt(n * sections)
    hbm = pl.BlockSpec(memory_space=pl.ANY)
    vmem = pl.BlockSpec(memory_space=pltpu.VMEM)
    dma = pltpu.SemaphoreType.DMA
    flops = 2 * fd * n * bs * sections * slots * 2 + 6 * full * full * npd
    results = pl.pallas_call(
        functools.partial(kernel, cols_n, scale),
        out_shape=(
            jax.ShapeDtypeStruct((fd, n), bf16),
            jax.ShapeDtypeStruct((fd, full), f32),
            jax.ShapeDtypeStruct((fd, n), bf16),
        ),
        in_specs=[pl.BlockSpec(memory_space=pltpu.SMEM)] * 2 + [hbm] * 4,
        out_specs=(hbm, vmem, vmem),
        scratch_shapes=[
            pltpu.VMEM(a_blocks.shape, bf16),
            pltpu.VMEM((2, fd, n), bf16),
            pltpu.VMEM((2, n // bs, fd, bs), bf16),
            pltpu.VMEM((nb, fd, bs), f32),
            pltpu.VMEM((cols_n, fd, npd), bf16),
            pltpu.VMEM((full, npd), bf16),
            pltpu.VMEM((full, full), bf16),
            pltpu.VMEM((full, full), bf16),
            pltpu.VMEM((full, npd), bf16),
            pltpu.VMEM((full, npd), bf16),
            pltpu.VMEM((full, npd), bf16),
            pltpu.VMEM((full, npd), bf16),
            pltpu.VMEM((fd, n), bf16),
            pltpu.VMEM((cols_n, 2, h, full), f32),
            pltpu.VMEM((cols_n, h, full), f32),
            pltpu.VMEM((hi, lo, h, full), bf16),
            pltpu.VMEM((lo, hi, h, full), bf16),
            pltpu.VMEM((hi, h, full), f32),
            pltpu.VMEM((hi, h, full), bf16),
            pltpu.VMEM((hi, h, full), bf16),
            pltpu.VMEM((h, full), f32),
            pltpu.VMEM((h, full), f32),
            pltpu.VMEM((nb * slots + 1, fd, bs), f32),
            pltpu.VMEM((nb, fd, bs), f32),
            pltpu.VMEM((nb, fd, bs), f32),
            pltpu.VMEM((8, 128), jnp.int32),
            pltpu.SMEM((8, 128), jnp.int32),
            dma((7,)),
        ] + [dma((cols_n,))] * 14 + [dma((lo,))] * 2 + [dma((hi, lo))] * 2 + [dma((4,))] * 2,
        compiler_params=pltpu.CompilerParams(
            collective_id=0, has_side_effects=True, vmem_limit_bytes=62 * 2**20
        ),
        cost_estimate=pl.CostEstimate(
            flops=flops, bytes_accessed=a_blocks.size * 2 + 8 * fd * n,
            transcendentals=full * npd,
        ),
    )(jnp.transpose(block_cols, (1, 2, 0)), block_counts.T, features, a_blocks, weight, cotangent)
    return pl.pallas_call(
        place,
        out_shape=tuple(jax.ShapeDtypeStruct(x.shape, x.dtype) for x in results),
        in_specs=[hbm] * 3,
        out_specs=(hbm,) * 3,
        scratch_shapes=[dma((3, 2))],
        compiler_params=pltpu.CompilerParams(vmem_limit_bytes=62 * 2**20),
        cost_estimate=pl.CostEstimate(
            flops=0, bytes_accessed=8 * fd * n + 8 * fd * full, transcendentals=0
        ),
    )(*results)


def place(*refs):
    sems = refs[6]
    copies = []
    for i in range(3):
        half = refs[i].shape[0] // 2
        for j in range(2):
            at = pl.ds(j * half, half)
            copies.append(
                pltpu.make_async_copy(refs[i].at[at], refs[i + 3].at[at], sems.at[i, j])
            )
    for copy in copies:
        copy.start()
    for copy in copies:
        copy.wait()


def local(rows_n, cols_n, features, a_blocks, block_cols, block_counts, weight, cotangent):
    fd, n = features.shape
    bs = a_blocks.shape[-1]
    args = (features, a_blocks, block_cols, block_counts, weight, cotangent)
    fits = (
        rows_n == 2
        and a_blocks.shape[1] == 2
        and a_blocks.shape[0] * bs == n
        and bs % 128 == 0
        and n % (cols_n * bs) == 0
        and fd % 32 == 0
        and a_blocks.shape[0] * a_blocks.shape[2] <= 128
        and a_blocks.shape[0] <= 128
        and 128 % fd == 0
        and weight.shape[1] % 128 == 0
        and weight.shape[1] == fd * cols_n
    )
    return fused(cols_n, *args) if fits else plain(*args)


def solution(mesh):
    placed = (
        P("col", "row"),
        P("row", None, None, None, None),
        P("row", None, None),
        P("row", None),
        P("col", None),
        P("col", "row"),
    )
    return jax.shard_map(
        functools.partial(local, mesh.shape["row"], mesh.shape["col"]),
        mesh=mesh,
        in_specs=placed,
        out_specs=(P("col", "row"), P("col", None), P("col", "row")),
        check_vma=False,
    )
```

```python
import functools
import math

import jax
import jax.numpy as jnp
from jax import lax
from jax.experimental import pallas as pl
from jax.experimental.pallas import tpu as pltpu
from jax.sharding import PartitionSpec as P

MESH = pl.DeviceIdType.MESH
f32 = jnp.float32
bf16 = jnp.bfloat16


def from_root(value, axis, source):
    kept = jnp.where(lax.axis_index(axis) == source, value, 0).astype(value.dtype)
    return lax.psum(kept, axis)


def plain(features, a_blocks, block_cols, block_counts, weight, cotangent):
    feat_dev = features.shape[0]
    slab_rows = features.shape[1]
    block_size = a_blocks.shape[-1]
    local_blocks = a_blocks.shape[0]
    section_count = a_blocks.shape[1]
    slot_count = a_blocks.shape[2]
    row_blocks = slab_rows // block_size
    slot_ids = jnp.arange(slot_count, dtype=jnp.int32)
    live_mask = (slot_ids[None, None, :] < block_counts[:, :, None]).astype(jnp.bfloat16)
    masked = a_blocks * live_mask[:, :, :, None, None]
    global_index = (
        jnp.arange(section_count, dtype=jnp.int32)[None, :, None] * row_blocks + block_cols
    )
    node_total = slab_rows * lax.axis_size("row")
    total = jnp.zeros((feat_dev, local_blocks, block_size), jnp.float32)
    for section_idx in range(lax.axis_size("row")):
        panel_rows = from_root(features, "row", section_idx).reshape(
            feat_dev, row_blocks, block_size
        )
        picked = panel_rows[:, block_cols[:, section_idx, :]]
        total = total + jnp.einsum(
            "fbkj,bkij->fbi", picked, masked[:, section_idx], preferred_element_type=jnp.float32
        )
    aggregated = total.reshape(feat_dev, slab_rows).astype(jnp.bfloat16)
    agg_full = lax.all_gather(aggregated, "col", axis=0, tiled=True)
    preact = jnp.dot(weight, agg_full, preferred_element_type=jnp.float32)
    output = jax.nn.silu(preact).astype(jnp.bfloat16)
    sigmoid_pre = jax.nn.sigmoid(preact)
    dpre = (
        cotangent.astype(jnp.float32) * sigmoid_pre * (1.0 + preact * (1.0 - sigmoid_pre))
    ).astype(jnp.bfloat16)
    local_grad = lax.dot_general(
        dpre, agg_full, (((1,), (1,)), ((), ())), preferred_element_type=jnp.float32
    )
    grad_weight = lax.psum(local_grad, "row") / jnp.sqrt(jnp.float32(node_total))
    dpre_full, weight_full = (
        lax.all_gather(dpre, "col", axis=0, tiled=True),
        lax.all_gather(weight, "col", axis=0, tiled=True),
    )
    first_col = lax.axis_index("col") * feat_dev
    weight_cols = lax.dynamic_slice_in_dim(weight_full, first_col, feat_dev, 1)
    dagg = lax.dot_general(
        weight_cols, dpre_full, (((0,), (0,)), ((), ())), preferred_element_type=jnp.float32
    ).astype(jnp.bfloat16)
    contrib = jnp.einsum(
        "fbi,bskij->fbskj",
        dagg.reshape(feat_dev, local_blocks, block_size),
        masked,
        preferred_element_type=jnp.float32,
    )
    terms = (
        jnp.zeros((feat_dev, section_count * row_blocks, block_size), jnp.float32)
        .at[:, global_index]
        .add(contrib)
    )
    terms = terms.reshape(feat_dev, section_count * slab_rows)
    grad_features = lax.psum_scatter(terms, "row", scatter_dimension=1, tiled=True).astype(
        jnp.bfloat16
    )
    return (output, grad_weight, grad_features)


NT = (((1,), (1,)), ((), ()))


def link_rows(block_cols, s, order, slots):
    lane = lax.broadcasted_iota(jnp.int32, (1, 128), 1)
    dest = jnp.full((1, 128), -1, jnp.int32)
    for i, b in enumerate(order):
        for k in range(slots):
            dest = jnp.where(lane == i * slots + k, block_cols[s, k, b], dest)
    across = jnp.broadcast_to(dest, (128, 128))
    down = across.T
    first = lax.broadcasted_iota(jnp.int32, (128, 128), 0)
    second = lax.broadcasted_iota(jnp.int32, (128, 128), 1)
    before = jnp.where((down == across) & (first < second), first + 1, 0)
    last = jnp.where(down == second, first + 1, 0)
    return jnp.max(before, axis=0, keepdims=True), jnp.max(last, axis=0, keepdims=True)


def kernel(
    cols_n, scale,
    block_cols, counts, feat, a, w, cot,
    out, gw, gf,
    av, fv, fb, acc, sagg, aggf, wf, wt, cotf, dpre, sout, sdag, rdag,
    gpart, grecv, gsend, gnear, gsum, gmid, gfar, grow, ghalf, chain, tsend, trecv, table_v, table,
    loc, cot_s, cot_r, w_s, w_r, wf_s, wf_r, agg_s, agg_r, out_s, out_r,
    dag_s, dag_r, gw_s, gw_r, gn_s, gn_r, wn_s, wn_r, pair_s, pair_r,
):
    me = lax.axis_index("col")
    r = lax.axis_index("row")
    o = 1 - r
    fd, n = feat.shape
    nb, sections, slots, bs, _ = a.shape
    full = wf.shape[0]
    npd = n // cols_n
    bpd = npd // bs
    h = fd // 2
    entries = nb * slots
    chunk = math.gcd(full, 128)

    def peer(d):
        return lax.rem(me + d, cols_n)

    def source(d):
        return lax.rem(me + cols_n - d, cols_n)

    def rows(c, size):
        return pl.ds(pl.multiple_of(c * size, size), size)

    def remote(src, dst, ss, rs, where):
        return pltpu.make_async_remote_copy(
            src_ref=src, dst_ref=dst, send_sem=ss, recv_sem=rs,
            device_id=where, device_id_type=MESH,
        )

    def each(fn):
        @pl.loop(1, cols_n)
        def _(d):
            fn(d)

    barrier = pltpu.get_barrier_semaphore()
    pl.semaphore_signal(barrier, inc=1, device_id={"row": o}, device_id_type=MESH)
    each(lambda d: pl.semaphore_signal(
        barrier, inc=1, device_id={"col": peer(d)}, device_id_type=MESH))

    own_feat = pltpu.make_async_copy(feat, fv.at[r], loc.at[0])
    own_a = pltpu.make_async_copy(a.at[:, r], av.at[:, r], loc.at[1])
    other_a = pltpu.make_async_copy(a.at[:, o], av.at[:, o], loc.at[2])
    own_w = pltpu.make_async_copy(w, wf.at[rows(me, fd)], loc.at[3])
    own_cot = pltpu.make_async_copy(cot.at[:, rows(me, npd)], cotf.at[rows(me, fd)], loc.at[4])
    own_feat.start()
    own_a.start()
    other_a.start()
    own_w.start()
    own_cot.start()
    pl.semaphore_wait(barrier, cols_n)

    swap = remote(feat, fv.at[r], pair_s.at[0], pair_r.at[0], {"row": o})
    swap_in = remote(feat, fv.at[o], pair_s.at[0], pair_r.at[0], {"row": o})
    swap.start()

    def half_rows(c, half):
        return pl.ds(pl.multiple_of(c * fd + half * h, h), h)

    lo = math.gcd(cols_n, 4)
    hi = cols_n // lo
    my_lo = lax.rem(me, lo)
    my_hi = me // lo

    def near(v):
        return my_hi * lo + lax.rem(my_lo + v, lo)

    def far(u):
        return lax.rem(my_hi + u, hi) * lo + my_lo

    def origin(u, v):
        return lax.rem(my_hi + hi - u, hi) * lo + lax.rem(my_lo + lo - v, lo)

    def w_far(u, c):
        return remote(w.at[rows(r, h)], wf.at[half_rows(c, r)], w_s.at[u], w_r.at[u],
                      {"col": far(u)})

    def w_near(u, v, c):
        part = wf.at[half_rows(c, r)]
        return remote(part, part, wn_s.at[u, v], wn_r.at[u, v], {"col": near(v)})

    def cot_copy(d, c):
        return remote(cot.at[:, rows(peer(d), npd)], cotf.at[rows(c, fd)], cot_s.at[d],
                      cot_r.at[d], {"col": peer(d)})

    def wf_copy(d, half):
        part = wf.at[half_rows(origin(d // lo, lax.rem(d, lo)), half)]
        return remote(part, part, wf_s.at[d], wf_r.at[d], {"row": o})

    def agg_copy(d, c):
        return remote(sagg.at[peer(d)], aggf.at[rows(c, fd)], agg_s.at[d], agg_r.at[d],
                      {"col": peer(d)})

    def out_copy(d, c):
        return remote(sout.at[rows(peer(d), fd)], out.at[:, rows(c, npd)], out_s.at[d],
                      out_r.at[d], {"col": peer(d)})

    def dag_copy(d, c):
        return remote(sdag.at[rows(peer(d), fd)], rdag.at[:, rows(c, npd)], dag_s.at[d],
                      dag_r.at[d], {"col": peer(d)})

    def gw_near(v):
        return remote(gsend.at[:, lax.rem(my_lo + v, lo)], gnear.at[v], gn_s.at[v], gn_r.at[v],
                      {"col": near(v)})

    def gw_far(u):
        return remote(gmid.at[lax.rem(my_hi + u, hi)], gfar.at[u], gw_s.at[u], gw_r.at[u],
                      {"col": far(u)})

    for u in range(1, hi):
        w_far(u, me).start()
    own_w.wait()
    for v in range(1, lo):
        w_near(0, v, me).start()
    each(lambda d: cot_copy(d, me).start())

    def alive(count, k):
        return jnp.minimum(jnp.maximum(count - k, 0), 1).astype(f32)

    def split_blocks(s):
        for c in range(nb):
            fb[s, c] = fv[s, :, c * bs:(c + 1) * bs]

    def gathered(b, s):
        picks = []
        count = counts[s, b]
        for k in range(slots):
            c = block_cols[s, k, b]
            picks.append((fb[s, c].astype(f32) * alive(count, k)).astype(bf16))
        left = jnp.concatenate(picks, axis=1)
        right = jnp.concatenate([av[b, s, k] for k in range(slots)], axis=1)
        return lax.dot_general(left, right, NT, preferred_element_type=f32)

    own_feat.wait()
    split_blocks(r)
    own_a.wait()

    @pl.loop(0, nb, unroll=4)
    def _(b):
        acc[b] = gathered(b, r)

    for u in range(1, hi):
        w_far(u, origin(u, 0)).wait_recv()
        for v in range(1, lo):
            w_near(u, v, origin(u, 0)).start()

    swap_in.wait_recv()
    split_blocks(o)
    other_a.wait()

    def finish(c):
        parts = []
        for j in range(bpd):
            b = c * bpd + j
            parts.append((acc[b] + gathered(b, o)).astype(bf16))
        return jnp.concatenate(parts, axis=1)

    def send_agg(d):
        sagg[peer(d)] = finish(peer(d))
        agg_copy(d, me).start()

    pl.loop(1, cols_n, unroll=3)(send_agg)
    aggf[rows(me, fd), :] = finish(me)

    for d in range(1, cols_n):
        u, v = d // lo, d % lo
        if v:
            w_near(u, v, origin(u, v)).wait_recv()
        wf_copy(d, r).start()
    order = [source(d) * bpd + j for d in range(cols_n) for j in range(bpd)]
    for s in range(sections):
        by_entry, by_block = link_rows(block_cols, s, order, slots)
        table_v[2 * s:2 * s + 1, :] = by_entry
        table_v[2 * s + 1:2 * s + 2, :] = by_block
    put_table = pltpu.make_async_copy(table_v, table, loc.at[6])
    put_table.start()
    each(lambda d: wf_copy(d, o).wait_recv())
    for q in range(full // chunk):
        wt[:, pl.ds(q * chunk, chunk)] = wf[pl.ds(q * chunk, chunk), :].T
    own_cot.wait()
    each(lambda d: cot_copy(d, source(d)).wait_recv())
    each(lambda d: agg_copy(d, source(d)).wait_recv())

    for q in range(full // chunk):
        at = pl.ds(q * chunk, chunk)
        pre = jnp.dot(wf[at, :], aggf[...], preferred_element_type=f32)
        sig = jax.nn.sigmoid(pre)
        sout[at, :] = (pre * sig).astype(bf16)
        dpre[at, :] = (cotf[at, :].astype(f32) * sig * (1.0 + pre * (1.0 - sig))).astype(bf16)
    for q in range(full // chunk):
        at = pl.ds(q * chunk, chunk)
        sdag[at, :] = jnp.dot(wt[at, :], dpre[...], preferred_element_type=f32).astype(bf16)

    each(lambda d: dag_copy(d, me).start())
    rdag[:, rows(me, npd)] = sdag[rows(me, fd), :]
    own_out = pltpu.make_async_copy(sout.at[rows(me, fd)], out.at[:, rows(me, npd)], loc.at[5])
    own_out.start()

    per_chunk = chunk // fd
    for q in range(full // chunk):
        part = lax.dot_general(dpre[pl.ds(q * chunk, chunk), :], aggf[...], NT,
                               preferred_element_type=f32) * scale
        gpart[pl.ds(q * per_chunk, per_chunk)] = part.reshape(per_chunk, 2, h, full)
    gswap = remote(gpart.at[:, o], grecv, pair_s.at[1], pair_r.at[1], {"row": o})
    gswap.start()
    gswap.wait_recv()

    @pl.loop(0, cols_n)
    def _(c):
        both = gpart[c, r] + grecv[c]
        grecv[c] = both
        gsend[c // lo, lax.rem(c, lo)] = both.astype(bf16)

    for v in range(1, lo):
        gw_near(v).start()
    each(lambda d: out_copy(d, me).start())

    put_table.wait()
    chain[0] = jnp.zeros(chain.shape[1:], f32)

    def blocks_of(s, d):
        for j in range(bpd):
            i = d * bpd + j
            b = source(d) * bpd + j
            count = counts[s, b]
            right = jnp.concatenate([av[b, s, k] for k in range(slots)], axis=1)
            terms = jnp.dot(rdag[:, pl.ds(pl.multiple_of(b * bs, bs), bs)], right,
                            preferred_element_type=f32)
            for k in range(slots):
                e = i * slots + k
                before = chain[table[2 * s, e]]
                chain[e + 1] = before + terms[:, k * bs:(k + 1) * bs] * alive(count, k)

    blocks_of(o, 0)

    @pl.loop(1, cols_n, unroll=3)
    def _(d):
        dag_copy(d, source(d)).wait_recv()
        blocks_of(o, d)


    @pl.loop(0, nb, unroll=4)
    def _(c):
        tsend[c] = chain[table[2 * o + 1, c]]

    tswap = remote(tsend, trecv, pair_s.at[2], pair_r.at[2], {"row": o})
    tswap.start()
    for v in range(1, lo):
        gw_near(v).wait_recv()
    for u in range(hi):
        level = grecv[u * lo + my_lo]
        for v in range(1, lo):
            level = level + gnear[v, u].astype(f32)
        gsum[u] = level
        gmid[u] = level.astype(bf16)
    for u in range(1, hi):
        gw_far(u).start()

    @pl.loop(0, cols_n, unroll=4)
    def _(d):
        blocks_of(r, d)

    tswap.wait_recv()

    @pl.loop(0, nb, unroll=4)
    def _(c):
        last = chain[table[2 * r + 1, c]]
        gf[:, pl.ds(pl.multiple_of(c * bs, bs), bs)] = (last + trecv[c]).astype(bf16)

    total = gsum[my_hi]
    for u in range(1, hi):
        gw_far(u).wait_recv()
        total = total + gfar[u].astype(f32)
    ghalf[...] = total
    gw[rows(r, h), :] = total
    rswap = remote(ghalf, grow, pair_s.at[3], pair_r.at[3], {"row": o})
    rswap.start()
    rswap.wait_recv()
    gw[rows(o, h), :] = grow[...]

    each(lambda d: out_copy(d, source(d)).wait_recv())
    own_out.wait()

    def drain(d):
        cot_copy(d, me).wait_send()
        wf_copy(d, r).wait_send()
        agg_copy(d, me).wait_send()
        dag_copy(d, me).wait_send()
        out_copy(d, me).wait_send()

    each(drain)
    for u in range(hi):
        for v in range(1, lo):
            w_near(u, v, origin(u, 0)).wait_send()
    for u in range(1, hi):
        w_far(u, me).wait_send()
        gw_far(u).wait_send()
    for v in range(1, lo):
        gw_near(v).wait_send()
    swap.wait_send()
    gswap.wait_send()
    tswap.wait_send()
    rswap.wait_send()


def fused(cols_n, features, a_blocks, block_cols, block_counts, weight, cotangent):
    fd, n = features.shape
    nb, sections, slots, bs, _ = a_blocks.shape
    full = weight.shape[1]
    npd = n // cols_n
    h = fd // 2
    lo = math.gcd(cols_n, 4)
    hi = cols_n // lo
    scale = 1.0 / math.sqrt(n * sections)
    hbm = pl.BlockSpec(memory_space=pl.ANY)
    vmem = pl.BlockSpec(memory_space=pltpu.VMEM)
    dma = pltpu.SemaphoreType.DMA
    flops = 2 * fd * n * bs * sections * slots * 2 + 6 * full * full * npd
    results = pl.pallas_call(
        functools.partial(kernel, cols_n, scale),
        out_shape=(
            jax.ShapeDtypeStruct((fd, n), bf16),
            jax.ShapeDtypeStruct((fd, full), f32),
            jax.ShapeDtypeStruct((fd, n), bf16),
        ),
        in_specs=[pl.BlockSpec(memory_space=pltpu.SMEM)] * 2 + [hbm] * 4,
        out_specs=(hbm, vmem, vmem),
        scratch_shapes=[
            pltpu.VMEM(a_blocks.shape, bf16),
            pltpu.VMEM((2, fd, n), bf16),
            pltpu.VMEM((2, n // bs, fd, bs), bf16),
            pltpu.VMEM((nb, fd, bs), f32),
            pltpu.VMEM((cols_n, fd, npd), bf16),
            pltpu.VMEM((full, npd), bf16),
            pltpu.VMEM((full, full), bf16),
            pltpu.VMEM((full, full), bf16),
            pltpu.VMEM((full, npd), bf16),
            pltpu.VMEM((full, npd), bf16),
            pltpu.VMEM((full, npd), bf16),
            pltpu.VMEM((full, npd), bf16),
            pltpu.VMEM((fd, n), bf16),
            pltpu.VMEM((cols_n, 2, h, full), f32),
            pltpu.VMEM((cols_n, h, full), f32),
            pltpu.VMEM((hi, lo, h, full), bf16),
            pltpu.VMEM((lo, hi, h, full), bf16),
            pltpu.VMEM((hi, h, full), f32),
            pltpu.VMEM((hi, h, full), bf16),
            pltpu.VMEM((hi, h, full), bf16),
            pltpu.VMEM((h, full), f32),
            pltpu.VMEM((h, full), f32),
            pltpu.VMEM((nb * slots + 1, fd, bs), f32),
            pltpu.VMEM((nb, fd, bs), f32),
            pltpu.VMEM((nb, fd, bs), f32),
            pltpu.VMEM((8, 128), jnp.int32),
            pltpu.SMEM((8, 128), jnp.int32),
            dma((7,)),
        ] + [dma((cols_n,))] * 14 + [dma((lo,))] * 2 + [dma((hi, lo))] * 2 + [dma((4,))] * 2,
        compiler_params=pltpu.CompilerParams(
            collective_id=0, has_side_effects=True, vmem_limit_bytes=62 * 2**20
        ),
        cost_estimate=pl.CostEstimate(
            flops=flops, bytes_accessed=a_blocks.size * 2 + 8 * fd * n,
            transcendentals=full * npd,
        ),
    )(jnp.transpose(block_cols, (1, 2, 0)), block_counts.T, features, a_blocks, weight, cotangent)
    return pl.pallas_call(
        place,
        out_shape=tuple(jax.ShapeDtypeStruct(x.shape, x.dtype) for x in results),
        in_specs=[hbm] * 3,
        out_specs=(hbm,) * 3,
        scratch_shapes=[pltpu.VMEM(x.shape, x.dtype) for x in results] + [dma((3, 2))],
        compiler_params=pltpu.CompilerParams(vmem_limit_bytes=62 * 2**20),
        cost_estimate=pl.CostEstimate(
            flops=0, bytes_accessed=8 * fd * n + 8 * fd * full, transcendentals=0
        ),
    )(*results)


def place(*refs):
    sems = refs[9]
    into = [pltpu.make_async_copy(refs[i], refs[i + 6], sems.at[i, 0]) for i in range(3)]
    back = [pltpu.make_async_copy(refs[i + 6], refs[i + 3], sems.at[i, 1]) for i in range(3)]
    for copy in into:
        copy.start()
    for i in range(3):
        into[i].wait()
        back[i].start()
    for copy in back:
        copy.wait()


def local(rows_n, cols_n, features, a_blocks, block_cols, block_counts, weight, cotangent):
    fd, n = features.shape
    bs = a_blocks.shape[-1]
    args = (features, a_blocks, block_cols, block_counts, weight, cotangent)
    fits = (
        rows_n == 2
        and a_blocks.shape[1] == 2
        and a_blocks.shape[0] * bs == n
        and bs % 128 == 0
        and n % (cols_n * bs) == 0
        and fd % 32 == 0
        and a_blocks.shape[0] * a_blocks.shape[2] <= 128
        and a_blocks.shape[0] <= 128
        and 128 % fd == 0
        and weight.shape[1] % 128 == 0
        and cols_n % 4 == 0
        and weight.shape[1] == fd * cols_n
    )
    return fused(cols_n, *args) if fits else plain(*args)


def solution(mesh):
    placed = (
        P("col", "row"),
        P("row", None, None, None, None),
        P("row", None, None),
        P("row", None),
        P("col", None),
        P("col", "row"),
    )
    return jax.shard_map(
        functools.partial(local, mesh.shape["row"], mesh.shape["col"]),
        mesh=mesh,
        in_specs=placed,
        out_specs=(P("col", "row"), P("col", None), P("col", "row")),
        check_vma=False,
    )
```

```python
import functools
import math

import jax
import jax.numpy as jnp
from jax import lax
from jax.experimental import pallas as pl
from jax.experimental.pallas import tpu as pltpu
from jax.sharding import PartitionSpec as P

MESH = pl.DeviceIdType.MESH
f32 = jnp.float32
bf16 = jnp.bfloat16


def from_root(value, axis, source):
    kept = jnp.where(lax.axis_index(axis) == source, value, 0).astype(value.dtype)
    return lax.psum(kept, axis)


def plain(features, a_blocks, block_cols, block_counts, weight, cotangent):
    feat_dev = features.shape[0]
    slab_rows = features.shape[1]
    block_size = a_blocks.shape[-1]
    local_blocks = a_blocks.shape[0]
    section_count = a_blocks.shape[1]
    slot_count = a_blocks.shape[2]
    row_blocks = slab_rows // block_size
    slot_ids = jnp.arange(slot_count, dtype=jnp.int32)
    live_mask = (slot_ids[None, None, :] < block_counts[:, :, None]).astype(jnp.bfloat16)
    masked = a_blocks * live_mask[:, :, :, None, None]
    global_index = (
        jnp.arange(section_count, dtype=jnp.int32)[None, :, None] * row_blocks + block_cols
    )
    node_total = slab_rows * lax.axis_size("row")
    total = jnp.zeros((feat_dev, local_blocks, block_size), jnp.float32)
    for section_idx in range(lax.axis_size("row")):
        panel_rows = from_root(features, "row", section_idx).reshape(
            feat_dev, row_blocks, block_size
        )
        picked = panel_rows[:, block_cols[:, section_idx, :]]
        total = total + jnp.einsum(
            "fbkj,bkij->fbi", picked, masked[:, section_idx], preferred_element_type=jnp.float32
        )
    aggregated = total.reshape(feat_dev, slab_rows).astype(jnp.bfloat16)
    agg_full = lax.all_gather(aggregated, "col", axis=0, tiled=True)
    preact = jnp.dot(weight, agg_full, preferred_element_type=jnp.float32)
    output = jax.nn.silu(preact).astype(jnp.bfloat16)
    sigmoid_pre = jax.nn.sigmoid(preact)
    dpre = (
        cotangent.astype(jnp.float32) * sigmoid_pre * (1.0 + preact * (1.0 - sigmoid_pre))
    ).astype(jnp.bfloat16)
    local_grad = lax.dot_general(
        dpre, agg_full, (((1,), (1,)), ((), ())), preferred_element_type=jnp.float32
    )
    grad_weight = lax.psum(local_grad, "row") / jnp.sqrt(jnp.float32(node_total))
    dpre_full, weight_full = (
        lax.all_gather(dpre, "col", axis=0, tiled=True),
        lax.all_gather(weight, "col", axis=0, tiled=True),
    )
    first_col = lax.axis_index("col") * feat_dev
    weight_cols = lax.dynamic_slice_in_dim(weight_full, first_col, feat_dev, 1)
    dagg = lax.dot_general(
        weight_cols, dpre_full, (((0,), (0,)), ((), ())), preferred_element_type=jnp.float32
    ).astype(jnp.bfloat16)
    contrib = jnp.einsum(
        "fbi,bskij->fbskj",
        dagg.reshape(feat_dev, local_blocks, block_size),
        masked,
        preferred_element_type=jnp.float32,
    )
    terms = (
        jnp.zeros((feat_dev, section_count * row_blocks, block_size), jnp.float32)
        .at[:, global_index]
        .add(contrib)
    )
    terms = terms.reshape(feat_dev, section_count * slab_rows)
    grad_features = lax.psum_scatter(terms, "row", scatter_dimension=1, tiled=True).astype(
        jnp.bfloat16
    )
    return (output, grad_weight, grad_features)


NT = (((1,), (1,)), ((), ()))


def link_rows(block_cols, s, order, slots):
    lane = lax.broadcasted_iota(jnp.int32, (1, 128), 1)
    dest = jnp.full((1, 128), -1, jnp.int32)
    for i, b in enumerate(order):
        for k in range(slots):
            dest = jnp.where(lane == i * slots + k, block_cols[s, k, b], dest)
    across = jnp.broadcast_to(dest, (128, 128))
    down = across.T
    first = lax.broadcasted_iota(jnp.int32, (128, 128), 0)
    second = lax.broadcasted_iota(jnp.int32, (128, 128), 1)
    before = jnp.where((down == across) & (first < second), first + 1, 0)
    last = jnp.where(down == second, first + 1, 0)
    return jnp.max(before, axis=0, keepdims=True), jnp.max(last, axis=0, keepdims=True)


def kernel(
    cols_n, scale,
    block_cols, counts, feat, a, w, cot,
    out, gw, gf,
    av, fv, fb, acc, sagg, aggf, wf, wt, cotf, dpre, sout, sdag, rdag,
    gpart, grecv, gsend, gnear, gsum, gmid, gfar, grow, ghalf, chain, tsend, trecv, table_v, table,
    loc, cot_s, cot_r, w_s, w_r, wf_s, wf_r, agg_s, agg_r, out_s, out_r,
    dag_s, dag_r, gw_s, gw_r, gn_s, gn_r, wn_s, wn_r, pair_s, pair_r,
):
    me = lax.axis_index("col")
    r = lax.axis_index("row")
    o = 1 - r
    fd, n = feat.shape
    nb, sections, slots, bs, _ = a.shape
    full = wf.shape[0]
    npd = n // cols_n
    bpd = npd // bs
    h = fd // 2
    entries = nb * slots
    chunk = math.gcd(full, 128)

    def peer(d):
        return lax.rem(me + d, cols_n)

    def source(d):
        return lax.rem(me + cols_n - d, cols_n)

    def rows(c, size):
        return pl.ds(pl.multiple_of(c * size, size), size)

    def remote(src, dst, ss, rs, where):
        return pltpu.make_async_remote_copy(
            src_ref=src, dst_ref=dst, send_sem=ss, recv_sem=rs,
            device_id=where, device_id_type=MESH,
        )

    def each(fn):
        @pl.loop(1, cols_n)
        def _(d):
            fn(d)

    barrier = pltpu.get_barrier_semaphore()
    pl.semaphore_signal(barrier, inc=1, device_id={"row": o}, device_id_type=MESH)
    each(lambda d: pl.semaphore_signal(
        barrier, inc=1, device_id={"col": peer(d)}, device_id_type=MESH))

    own_feat = pltpu.make_async_copy(feat, fv.at[r], loc.at[0])
    own_a = pltpu.make_async_copy(a.at[:, r], av.at[:, r], loc.at[1])
    other_a = pltpu.make_async_copy(a.at[:, o], av.at[:, o], loc.at[2])
    own_w = pltpu.make_async_copy(w, wf.at[rows(me, fd)], loc.at[3])
    own_cot = pltpu.make_async_copy(cot.at[:, rows(me, npd)], cotf.at[rows(me, fd)], loc.at[4])
    own_feat.start()
    own_a.start()
    other_a.start()
    own_w.start()
    own_cot.start()
    pl.semaphore_wait(barrier, cols_n)

    swap = remote(feat, fv.at[r], pair_s.at[0], pair_r.at[0], {"row": o})
    swap_in = remote(feat, fv.at[o], pair_s.at[0], pair_r.at[0], {"row": o})
    swap.start()

    def half_rows(c, half):
        return pl.ds(pl.multiple_of(c * fd + half * h, h), h)

    lo = math.gcd(cols_n, 4)
    hi = cols_n // lo
    my_lo = lax.rem(me, lo)
    my_hi = me // lo

    def near(v):
        return my_hi * lo + lax.rem(my_lo + v, lo)

    def far(u):
        return lax.rem(my_hi + u, hi) * lo + my_lo

    def origin(u, v):
        return lax.rem(my_hi + hi - u, hi) * lo + lax.rem(my_lo + lo - v, lo)

    def w_far(u, c):
        return remote(w.at[rows(r, h)], wf.at[half_rows(c, r)], w_s.at[u], w_r.at[u],
                      {"col": far(u)})

    def w_near(u, v, c):
        part = wf.at[half_rows(c, r)]
        return remote(part, part, wn_s.at[u, v], wn_r.at[u, v], {"col": near(v)})

    def cot_copy(d, c):
        return remote(cot.at[:, rows(peer(d), npd)], cotf.at[rows(c, fd)], cot_s.at[d],
                      cot_r.at[d], {"col": peer(d)})

    def wf_copy(d, half):
        part = wf.at[half_rows(origin(d // lo, lax.rem(d, lo)), half)]
        return remote(part, part, wf_s.at[d], wf_r.at[d], {"row": o})

    def agg_copy(j, d, c):
        return remote(sagg.at[j, peer(d)], aggf.at[j, rows(c, fd)], agg_s.at[j, d],
                      agg_r.at[j, d], {"col": peer(d)})

    def out_copy(j, d, c):
        return remote(sout.at[j, rows(peer(d), fd)], out.at[:, rows(c * bpd + j, bs)],
                      out_s.at[j, d], out_r.at[j, d], {"col": peer(d)})

    def dag_copy(j, d, c):
        return remote(sdag.at[j, rows(peer(d), fd)], rdag.at[j, c], dag_s.at[j, d],
                      dag_r.at[j, d], {"col": peer(d)})

    def gw_near(v):
        return remote(gsend.at[:, lax.rem(my_lo + v, lo)], gnear.at[v], gn_s.at[v], gn_r.at[v],
                      {"col": near(v)})

    def gw_far(u):
        return remote(gmid.at[lax.rem(my_hi + u, hi)], gfar.at[u], gw_s.at[u], gw_r.at[u],
                      {"col": far(u)})

    for u in range(1, hi):
        w_far(u, me).start()
    own_w.wait()
    for v in range(1, lo):
        w_near(0, v, me).start()
    each(lambda d: cot_copy(d, me).start())

    def alive(count, k):
        return jnp.minimum(jnp.maximum(count - k, 0), 1).astype(f32)

    def split_blocks(s):
        for c in range(nb):
            fb[s, c] = fv[s, :, c * bs:(c + 1) * bs]

    def gathered(b, s):
        picks = []
        count = counts[s, b]
        for k in range(slots):
            c = block_cols[s, k, b]
            picks.append((fb[s, c].astype(f32) * alive(count, k)).astype(bf16))
        left = jnp.concatenate(picks, axis=1)
        right = jnp.concatenate([av[b, s, k] for k in range(slots)], axis=1)
        return lax.dot_general(left, right, NT, preferred_element_type=f32)

    own_feat.wait()
    split_blocks(r)
    own_a.wait()

    @pl.loop(0, nb, unroll=4)
    def _(b):
        acc[b] = gathered(b, r)

    for u in range(1, hi):
        w_far(u, origin(u, 0)).wait_recv()
        for v in range(1, lo):
            w_near(u, v, origin(u, 0)).start()

    swap_in.wait_recv()
    split_blocks(o)
    other_a.wait()

    def finish(j, c):
        b = c * bpd + j
        return (acc[b] + gathered(b, o)).astype(bf16)

    def forward_w():
        for d in range(1, cols_n):
            u, v = d // lo, d % lo
            if v:
                w_near(u, v, origin(u, v)).wait_recv()
            wf_copy(d, r).start()

    for j in range(bpd):
        @pl.loop(1, cols_n, unroll=5)
        def _(d, j=j):
            sagg[j, peer(d)] = finish(j, peer(d))
            agg_copy(j, d, me).start()

        aggf[j, rows(me, fd), :] = finish(j, me)
        if j == 0:
            forward_w()

    order = [source(d) * bpd + j for j in range(bpd) for d in range(cols_n)]
    for s in range(sections):
        by_entry, by_block = link_rows(block_cols, s, order, slots)
        table_v[2 * s:2 * s + 1, :] = by_entry
        table_v[2 * s + 1:2 * s + 2, :] = by_block
    put_table = pltpu.make_async_copy(table_v, table, loc.at[6])
    put_table.start()
    each(lambda d: wf_copy(d, o).wait_recv())
    for q in range(full // chunk):
        wt[:, pl.ds(q * chunk, chunk)] = wf[pl.ds(q * chunk, chunk), :].T
    own_cot.wait()
    each(lambda d: cot_copy(d, source(d)).wait_recv())
    own_out = []
    for j in range(bpd):
        each(lambda d: agg_copy(j, d, source(d)).wait_recv())
        span = pl.ds(j * bs, bs)
        for q in range(full // chunk):
            at = pl.ds(q * chunk, chunk)
            pre = jnp.dot(wf[at, :], aggf[j], preferred_element_type=f32)
            sig = jax.nn.sigmoid(pre)
            sout[j, at, :] = (pre * sig).astype(bf16)
            dpre[at, span] = (
                cotf[at, span].astype(f32) * sig * (1.0 + pre * (1.0 - sig))
            ).astype(bf16)
        for q in range(full // chunk):
            at = pl.ds(q * chunk, chunk)
            sdag[j, at, :] = jnp.dot(
                wt[at, :], dpre[:, span], preferred_element_type=f32
            ).astype(bf16)
        each(lambda d: dag_copy(j, d, me).start())
        if j < bpd - 1:
            each(lambda d: out_copy(j, d, me).start())
        rdag[j, me] = sdag[j, rows(me, fd), :]
        own_out.append(pltpu.make_async_copy(
            sout.at[j, rows(me, fd)], out.at[:, rows(me * bpd + j, bs)], loc.at[7 + j]))
        own_out[j].start()

    per_chunk = chunk // fd
    for q in range(full // chunk):
        right = jnp.concatenate([aggf[j] for j in range(bpd)], axis=1)
        part = lax.dot_general(dpre[pl.ds(q * chunk, chunk), :], right, NT,
                               preferred_element_type=f32) * scale
        gpart[pl.ds(q * per_chunk, per_chunk)] = part.reshape(per_chunk, 2, h, full)
    gswap = remote(gpart.at[:, o], grecv, pair_s.at[1], pair_r.at[1], {"row": o})
    gswap.start()
    gswap.wait_recv()

    @pl.loop(0, cols_n)
    def _(c):
        both = gpart[c, r] + grecv[c]
        grecv[c] = both
        gsend[c // lo, lax.rem(c, lo)] = both.astype(bf16)

    for v in range(1, lo):
        gw_near(v).start()
    each(lambda d: out_copy(bpd - 1, d, me).start())

    put_table.wait()
    chain[0] = jnp.zeros(chain.shape[1:], f32)

    def block_of(s, j, d):
        i = j * cols_n + d
        b = source(d) * bpd + j
        count = counts[s, b]
        right = jnp.concatenate([av[b, s, k] for k in range(slots)], axis=1)
        terms = jnp.dot(rdag[j, source(d)], right, preferred_element_type=f32)
        for k in range(slots):
            e = i * slots + k
            before = chain[table[2 * s, e]]
            chain[e + 1] = before + terms[:, k * bs:(k + 1) * bs] * alive(count, k)

    for j in range(bpd):
        block_of(o, j, 0)

        @pl.loop(1, cols_n, unroll=5)
        def _(d, j=j):
            dag_copy(j, d, source(d)).wait_recv()
            block_of(o, j, d)

    @pl.loop(0, nb, unroll=4)
    def _(c):
        tsend[c] = chain[table[2 * o + 1, c]]

    tswap = remote(tsend, trecv, pair_s.at[2], pair_r.at[2], {"row": o})
    tswap.start()
    for v in range(1, lo):
        gw_near(v).wait_recv()
    for u in range(hi):
        level = grecv[u * lo + my_lo]
        for v in range(1, lo):
            level = level + gnear[v, u].astype(f32)
        gsum[u] = level
        gmid[u] = level.astype(bf16)
    for u in range(1, hi):
        gw_far(u).start()

    for j in range(bpd):
        @pl.loop(0, cols_n, unroll=4)
        def _(d, j=j):
            block_of(r, j, d)

    tswap.wait_recv()

    @pl.loop(0, nb, unroll=4)
    def _(c):
        last = chain[table[2 * r + 1, c]]
        gf[:, pl.ds(pl.multiple_of(c * bs, bs), bs)] = (last + trecv[c]).astype(bf16)

    total = gsum[my_hi]
    for u in range(1, hi):
        gw_far(u).wait_recv()
        total = total + gfar[u].astype(f32)
    ghalf[...] = total
    gw[rows(r, h), :] = total
    rswap = remote(ghalf, grow, pair_s.at[3], pair_r.at[3], {"row": o})
    rswap.start()
    rswap.wait_recv()
    gw[rows(o, h), :] = grow[...]

    for j in range(bpd):
        each(lambda d: out_copy(j, d, source(d)).wait_recv())
        own_out[j].wait()

    def drain(d):
        cot_copy(d, me).wait_send()
        wf_copy(d, r).wait_send()
        for j in range(bpd):
            agg_copy(j, d, me).wait_send()
            dag_copy(j, d, me).wait_send()
            out_copy(j, d, me).wait_send()

    each(drain)
    for u in range(hi):
        for v in range(1, lo):
            w_near(u, v, origin(u, 0)).wait_send()
    for u in range(1, hi):
        w_far(u, me).wait_send()
        gw_far(u).wait_send()
    for v in range(1, lo):
        gw_near(v).wait_send()
    swap.wait_send()
    gswap.wait_send()
    tswap.wait_send()
    rswap.wait_send()


def fused(cols_n, features, a_blocks, block_cols, block_counts, weight, cotangent):
    fd, n = features.shape
    nb, sections, slots, bs, _ = a_blocks.shape
    full = weight.shape[1]
    npd = n // cols_n
    h = fd // 2
    lo = math.gcd(cols_n, 4)
    hi = cols_n // lo
    bpd = npd // bs
    scale = 1.0 / math.sqrt(n * sections)
    hbm = pl.BlockSpec(memory_space=pl.ANY)
    vmem = pl.BlockSpec(memory_space=pltpu.VMEM)
    dma = pltpu.SemaphoreType.DMA
    flops = 2 * fd * n * bs * sections * slots * 2 + 6 * full * full * npd
    results = pl.pallas_call(
        functools.partial(kernel, cols_n, scale),
        out_shape=(
            jax.ShapeDtypeStruct((fd, n), bf16),
            jax.ShapeDtypeStruct((fd, full), f32),
            jax.ShapeDtypeStruct((fd, n), bf16),
        ),
        in_specs=[pl.BlockSpec(memory_space=pltpu.SMEM)] * 2 + [hbm] * 4,
        out_specs=(hbm, vmem, vmem),
        scratch_shapes=[
            pltpu.VMEM(a_blocks.shape, bf16),
            pltpu.VMEM((2, fd, n), bf16),
            pltpu.VMEM((2, n // bs, fd, bs), bf16),
            pltpu.VMEM((nb, fd, bs), f32),
            pltpu.VMEM((bpd, cols_n, fd, bs), bf16),
            pltpu.VMEM((bpd, full, bs), bf16),
            pltpu.VMEM((full, full), bf16),
            pltpu.VMEM((full, full), bf16),
            pltpu.VMEM((full, npd), bf16),
            pltpu.VMEM((full, npd), bf16),
            pltpu.VMEM((bpd, full, bs), bf16),
            pltpu.VMEM((bpd, full, bs), bf16),
            pltpu.VMEM((bpd, cols_n, fd, bs), bf16),
            pltpu.VMEM((cols_n, 2, h, full), f32),
            pltpu.VMEM((cols_n, h, full), f32),
            pltpu.VMEM((hi, lo, h, full), bf16),
            pltpu.VMEM((lo, hi, h, full), bf16),
            pltpu.VMEM((hi, h, full), f32),
            pltpu.VMEM((hi, h, full), bf16),
            pltpu.VMEM((hi, h, full), bf16),
            pltpu.VMEM((h, full), f32),
            pltpu.VMEM((h, full), f32),
            pltpu.VMEM((nb * slots + 1, fd, bs), f32),
            pltpu.VMEM((nb, fd, bs), f32),
            pltpu.VMEM((nb, fd, bs), f32),
            pltpu.VMEM((8, 128), jnp.int32),
            pltpu.SMEM((8, 128), jnp.int32),
            dma((7 + bpd,)),
        ] + [dma((cols_n,))] * 6 + [dma((bpd, cols_n))] * 6 + [dma((cols_n,))] * 2 + [dma((lo,))] * 2 + [dma((hi, lo))] * 2 + [dma((4,))] * 2,
        compiler_params=pltpu.CompilerParams(
            collective_id=0, has_side_effects=True, vmem_limit_bytes=62 * 2**20
        ),
        cost_estimate=pl.CostEstimate(
            flops=flops, bytes_accessed=a_blocks.size * 2 + 8 * fd * n,
            transcendentals=full * npd,
        ),
    )(jnp.transpose(block_cols, (1, 2, 0)), block_counts.T, features, a_blocks, weight, cotangent)
    return pl.pallas_call(
        place,
        out_shape=tuple(jax.ShapeDtypeStruct(x.shape, x.dtype) for x in results),
        in_specs=[hbm] * 3,
        out_specs=(hbm,) * 3,
        scratch_shapes=[pltpu.VMEM(x.shape, x.dtype) for x in results] + [dma((3, 2))],
        compiler_params=pltpu.CompilerParams(vmem_limit_bytes=62 * 2**20),
        cost_estimate=pl.CostEstimate(
            flops=0, bytes_accessed=8 * fd * n + 8 * fd * full, transcendentals=0
        ),
    )(*results)


def place(*refs):
    sems = refs[9]
    into = [pltpu.make_async_copy(refs[i], refs[i + 6], sems.at[i, 0]) for i in range(3)]
    back = [pltpu.make_async_copy(refs[i + 6], refs[i + 3], sems.at[i, 1]) for i in range(3)]
    for copy in into:
        copy.start()
    for i in range(3):
        into[i].wait()
        back[i].start()
    for copy in back:
        copy.wait()


def local(rows_n, cols_n, features, a_blocks, block_cols, block_counts, weight, cotangent):
    fd, n = features.shape
    bs = a_blocks.shape[-1]
    args = (features, a_blocks, block_cols, block_counts, weight, cotangent)
    fits = (
        rows_n == 2
        and a_blocks.shape[1] == 2
        and a_blocks.shape[0] * bs == n
        and bs % 128 == 0
        and n % (cols_n * bs) == 0
        and fd % 32 == 0
        and a_blocks.shape[0] * a_blocks.shape[2] <= 128
        and a_blocks.shape[0] <= 128
        and 128 % fd == 0
        and weight.shape[1] % 128 == 0
        and cols_n % 4 == 0
        and weight.shape[1] == fd * cols_n
    )
    return fused(cols_n, *args) if fits else plain(*args)


def solution(mesh):
    placed = (
        P("col", "row"),
        P("row", None, None, None, None),
        P("row", None, None),
        P("row", None),
        P("col", None),
        P("col", "row"),
    )
    return jax.shard_map(
        functools.partial(local, mesh.shape["row"], mesh.shape["col"]),
        mesh=mesh,
        in_specs=placed,
        out_specs=(P("col", "row"), P("col", None), P("col", "row")),
        check_vma=False,
    )
```

```python
import functools
import math

import jax
import jax.numpy as jnp
from jax import lax
from jax.experimental import pallas as pl
from jax.experimental.pallas import tpu as pltpu
from jax.sharding import PartitionSpec as P

MESH = pl.DeviceIdType.MESH
f32 = jnp.float32
bf16 = jnp.bfloat16


def from_root(value, axis, source):
    kept = jnp.where(lax.axis_index(axis) == source, value, 0).astype(value.dtype)
    return lax.psum(kept, axis)


def plain(features, a_blocks, block_cols, block_counts, weight, cotangent):
    feat_dev = features.shape[0]
    slab_rows = features.shape[1]
    block_size = a_blocks.shape[-1]
    local_blocks = a_blocks.shape[0]
    section_count = a_blocks.shape[1]
    slot_count = a_blocks.shape[2]
    row_blocks = slab_rows // block_size
    slot_ids = jnp.arange(slot_count, dtype=jnp.int32)
    live_mask = (slot_ids[None, None, :] < block_counts[:, :, None]).astype(jnp.bfloat16)
    masked = a_blocks * live_mask[:, :, :, None, None]
    global_index = (
        jnp.arange(section_count, dtype=jnp.int32)[None, :, None] * row_blocks + block_cols
    )
    node_total = slab_rows * lax.axis_size("row")
    total = jnp.zeros((feat_dev, local_blocks, block_size), jnp.float32)
    for section_idx in range(lax.axis_size("row")):
        panel_rows = from_root(features, "row", section_idx).reshape(
            feat_dev, row_blocks, block_size
        )
        picked = panel_rows[:, block_cols[:, section_idx, :]]
        total = total + jnp.einsum(
            "fbkj,bkij->fbi", picked, masked[:, section_idx], preferred_element_type=jnp.float32
        )
    aggregated = total.reshape(feat_dev, slab_rows).astype(jnp.bfloat16)
    agg_full = lax.all_gather(aggregated, "col", axis=0, tiled=True)
    preact = jnp.dot(weight, agg_full, preferred_element_type=jnp.float32)
    output = jax.nn.silu(preact).astype(jnp.bfloat16)
    sigmoid_pre = jax.nn.sigmoid(preact)
    dpre = (
        cotangent.astype(jnp.float32) * sigmoid_pre * (1.0 + preact * (1.0 - sigmoid_pre))
    ).astype(jnp.bfloat16)
    local_grad = lax.dot_general(
        dpre, agg_full, (((1,), (1,)), ((), ())), preferred_element_type=jnp.float32
    )
    grad_weight = lax.psum(local_grad, "row") / jnp.sqrt(jnp.float32(node_total))
    dpre_full, weight_full = (
        lax.all_gather(dpre, "col", axis=0, tiled=True),
        lax.all_gather(weight, "col", axis=0, tiled=True),
    )
    first_col = lax.axis_index("col") * feat_dev
    weight_cols = lax.dynamic_slice_in_dim(weight_full, first_col, feat_dev, 1)
    dagg = lax.dot_general(
        weight_cols, dpre_full, (((0,), (0,)), ((), ())), preferred_element_type=jnp.float32
    ).astype(jnp.bfloat16)
    contrib = jnp.einsum(
        "fbi,bskij->fbskj",
        dagg.reshape(feat_dev, local_blocks, block_size),
        masked,
        preferred_element_type=jnp.float32,
    )
    terms = (
        jnp.zeros((feat_dev, section_count * row_blocks, block_size), jnp.float32)
        .at[:, global_index]
        .add(contrib)
    )
    terms = terms.reshape(feat_dev, section_count * slab_rows)
    grad_features = lax.psum_scatter(terms, "row", scatter_dimension=1, tiled=True).astype(
        jnp.bfloat16
    )
    return (output, grad_weight, grad_features)


NT = (((1,), (1,)), ((), ()))


def link_rows(block_cols, s, order, slots):
    lane = lax.broadcasted_iota(jnp.int32, (1, 128), 1)
    dest = jnp.full((1, 128), -1, jnp.int32)
    for i, b in enumerate(order):
        for k in range(slots):
            dest = jnp.where(lane == i * slots + k, block_cols[s, k, b], dest)
    across = jnp.broadcast_to(dest, (128, 128))
    down = across.T
    first = lax.broadcasted_iota(jnp.int32, (128, 128), 0)
    second = lax.broadcasted_iota(jnp.int32, (128, 128), 1)
    before = jnp.where((down == across) & (first < second), first + 1, 0)
    last = jnp.where(down == second, first + 1, 0)
    return jnp.max(before, axis=0, keepdims=True), jnp.max(last, axis=0, keepdims=True)


def kernel(
    cols_n, scale,
    block_cols, counts, feat, a, w, cot,
    out, gw, gf,
    av, fv, fb, acc, sagg, aggf, wh, wf, wt, cotf, dpre, sout, sdag, rdag,
    gpart, grecv, gsend, gnear, gsum, gmid, gfar, grow, ghalf, chain, tsend, trecv, table_v, table,
    loc, cot_s, cot_r, w_s, w_r, wf_s, wf_r, agg_s, agg_r, out_s, out_r,
    dag_s, dag_r, gw_s, gw_r, gn_s, gn_r, wn_s, wn_r, pair_s, pair_r,
):
    me = lax.axis_index("col")
    r = lax.axis_index("row")
    o = 1 - r
    fd, n = feat.shape
    nb, sections, slots, bs, _ = a.shape
    full = wf.shape[0]
    npd = n // cols_n
    bpd = npd // bs
    h = fd // 2
    entries = nb * slots
    chunk = math.gcd(full, 128)

    def peer(d):
        return lax.rem(me + d, cols_n)

    def source(d):
        return lax.rem(me + cols_n - d, cols_n)

    def rows(c, size):
        return pl.ds(pl.multiple_of(c * size, size), size)

    def remote(src, dst, ss, rs, where):
        return pltpu.make_async_remote_copy(
            src_ref=src, dst_ref=dst, send_sem=ss, recv_sem=rs,
            device_id=where, device_id_type=MESH,
        )

    def each(fn):
        @pl.loop(1, cols_n)
        def _(d):
            fn(d)

    barrier = pltpu.get_barrier_semaphore()
    pl.semaphore_signal(barrier, inc=1, device_id={"row": o}, device_id_type=MESH)
    each(lambda d: pl.semaphore_signal(
        barrier, inc=1, device_id={"col": peer(d)}, device_id_type=MESH))

    own_feat = pltpu.make_async_copy(feat, fv.at[r], loc.at[0])
    own_a = pltpu.make_async_copy(a.at[:, r], av.at[:, r], loc.at[1])
    other_a = pltpu.make_async_copy(a.at[:, o], av.at[:, o], loc.at[2])
    own_w = pltpu.make_async_copy(w.at[rows(r, h)], wh.at[r, me], loc.at[3])
    own_cot = pltpu.make_async_copy(cot.at[:, rows(me, npd)], cotf.at[rows(me, fd)], loc.at[4])
    own_feat.start()
    own_a.start()
    other_a.start()
    own_w.start()
    own_cot.start()
    pl.semaphore_wait(barrier, cols_n)

    swap = remote(feat, fv.at[r], pair_s.at[0], pair_r.at[0], {"row": o})
    swap_in = remote(feat, fv.at[o], pair_s.at[0], pair_r.at[0], {"row": o})
    swap.start()

    lo = math.gcd(cols_n, 4)
    hi = cols_n // lo
    my_lo = lax.rem(me, lo)
    my_hi = me // lo

    def near(v):
        return my_hi * lo + lax.rem(my_lo + v, lo)

    def far(u):
        return lax.rem(my_hi + u, hi) * lo + my_lo

    def origin(u, v):
        return lax.rem(my_hi + hi - u, hi) * lo + lax.rem(my_lo + lo - v, lo)

    def w_far(u, c):
        return remote(w.at[rows(r, h)], wh.at[r, c], w_s.at[u], w_r.at[u],
                      {"col": far(u)})

    def w_near(u, v, c):
        part = wh.at[r, c]
        return remote(part, part, wn_s.at[u, v], wn_r.at[u, v], {"col": near(v)})

    def cot_copy(d, c):
        return remote(cot.at[:, rows(peer(d), npd)], cotf.at[rows(c, fd)], cot_s.at[0],
                      cot_r.at[0], {"col": peer(d)})

    def bulk(ref, ss, rs):
        part = ref.at[pl.ds(0, (cols_n - 1) * fd)]
        return remote(part, part, ss.at[0], rs.at[0], {"row": o})

    def half_copy(half):
        return remote(wh.at[half], wh.at[half], wf_s.at[0], wf_r.at[0], {"row": o})

    def agg_copy(d, c):
        return remote(sagg.at[peer(d)], aggf.at[rows(c, fd)], agg_s.at[0], agg_r.at[0],
                      {"col": peer(d)})

    def out_copy(d, c):
        return remote(sout.at[rows(peer(d), fd)], out.at[:, rows(c, npd)], out_s.at[0],
                      out_r.at[0], {"col": peer(d)})

    def dag_copy(d, c):
        return remote(sdag.at[rows(peer(d), fd)], rdag.at[:, rows(c, npd)], dag_s.at[0],
                      dag_r.at[d], {"col": peer(d)})

    def gw_near(v):
        return remote(gsend.at[:, lax.rem(my_lo + v, lo)], gnear.at[v], gn_s.at[v], gn_r.at[v],
                      {"col": near(v)})

    def gw_far(u):
        return remote(gmid.at[lax.rem(my_hi + u, hi)], gfar.at[u], gw_s.at[u], gw_r.at[u],
                      {"col": far(u)})

    for u in range(1, hi):
        w_far(u, me).start()
    own_w.wait()
    for v in range(1, lo):
        w_near(0, v, me).start()
    each(lambda d: cot_copy(d, me).start())

    def alive(count, k):
        return jnp.minimum(jnp.maximum(count - k, 0), 1).astype(f32)

    def split_blocks(s):
        for c in range(nb):
            fb[s, c] = fv[s, :, c * bs:(c + 1) * bs]

    def gathered(b, s):
        picks = []
        count = counts[s, b]
        for k in range(slots):
            c = block_cols[s, k, b]
            picks.append((fb[s, c].astype(f32) * alive(count, k)).astype(bf16))
        left = jnp.concatenate(picks, axis=1)
        right = jnp.concatenate([av[b, s, k] for k in range(slots)], axis=1)
        return lax.dot_general(left, right, NT, preferred_element_type=f32)

    own_feat.wait()
    split_blocks(r)
    own_a.wait()

    @pl.loop(0, nb, unroll=4)
    def _(b):
        acc[b] = gathered(b, r)

    for u in range(1, hi):
        w_far(u, origin(u, 0)).wait_recv()
        for v in range(1, lo):
            w_near(u, v, origin(u, 0)).start()

    swap_in.wait_recv()
    split_blocks(o)
    other_a.wait()

    def finish(c):
        parts = []
        for j in range(bpd):
            b = c * bpd + j
            parts.append((acc[b] + gathered(b, o)).astype(bf16))
        return jnp.concatenate(parts, axis=1)

    def send_agg(d):
        sagg[peer(d)] = finish(peer(d))
        agg_copy(d, me).start()

    pl.loop(1, cols_n, unroll=3)(send_agg)
    aggf[rows(me, fd), :] = finish(me)

    for d in range(1, cols_n):
        u, v = d // lo, d % lo
        if v:
            w_near(u, v, origin(u, v)).wait_recv()
    half_copy(r).start()
    order = [source(d) * bpd + j for d in range(cols_n) for j in range(bpd)]
    for s in range(sections):
        by_entry, by_block = link_rows(block_cols, s, order, slots)
        table_v[2 * s:2 * s + 1, :] = by_entry
        table_v[2 * s + 1:2 * s + 2, :] = by_block
    put_table = pltpu.make_async_copy(table_v, table, loc.at[6])
    put_table.start()
    half_copy(o).wait_recv()
    for c in range(cols_n):
        for half in range(2):
            wf[pl.ds(c * fd + half * h, h), :] = wh[half, c]
    for q in range(full // chunk):
        wt[:, pl.ds(q * chunk, chunk)] = wf[pl.ds(q * chunk, chunk), :].T
    own_cot.wait()
    bulk(cotf, cot_s, cot_r).wait_recv()
    bulk(aggf, agg_s, agg_r).wait_recv()

    for q in range(full // chunk):
        at = pl.ds(q * chunk, chunk)
        pre = jnp.dot(wf[at, :], aggf[...], preferred_element_type=f32)
        sig = jax.nn.sigmoid(pre)
        sout[at, :] = (pre * sig).astype(bf16)
        dpre[at, :] = (cotf[at, :].astype(f32) * sig * (1.0 + pre * (1.0 - sig))).astype(bf16)
    for q in range(full // chunk):
        at = pl.ds(q * chunk, chunk)
        sdag[at, :] = jnp.dot(wt[at, :], dpre[...], preferred_element_type=f32).astype(bf16)

    each(lambda d: dag_copy(d, me).start())
    rdag[:, rows(me, npd)] = sdag[rows(me, fd), :]
    own_out = pltpu.make_async_copy(sout.at[rows(me, fd)], out.at[:, rows(me, npd)], loc.at[5])
    own_out.start()

    per_chunk = chunk // fd
    for q in range(full // chunk):
        part = lax.dot_general(dpre[pl.ds(q * chunk, chunk), :], aggf[...], NT,
                               preferred_element_type=f32) * scale
        gpart[pl.ds(q * per_chunk, per_chunk)] = part.reshape(per_chunk, 2, h, full)
    gswap = remote(gpart.at[:, o], grecv, pair_s.at[1], pair_r.at[1], {"row": o})
    gswap.start()
    gswap.wait_recv()

    @pl.loop(0, cols_n)
    def _(c):
        both = gpart[c, r] + grecv[c]
        grecv[c] = both
        gsend[c // lo, lax.rem(c, lo)] = both.astype(bf16)

    for v in range(1, lo):
        gw_near(v).start()
    each(lambda d: out_copy(d, me).start())

    put_table.wait()
    chain[0] = jnp.zeros(chain.shape[1:], f32)

    def blocks_of(s, d):
        for j in range(bpd):
            i = d * bpd + j
            b = source(d) * bpd + j
            count = counts[s, b]
            right = jnp.concatenate([av[b, s, k] for k in range(slots)], axis=1)
            terms = jnp.dot(rdag[:, pl.ds(pl.multiple_of(b * bs, bs), bs)], right,
                            preferred_element_type=f32)
            for k in range(slots):
                e = i * slots + k
                before = chain[table[2 * s, e]]
                chain[e + 1] = before + terms[:, k * bs:(k + 1) * bs] * alive(count, k)

    blocks_of(o, 0)

    @pl.loop(1, cols_n, unroll=3)
    def _(d):
        dag_copy(d, source(d)).wait_recv()
        blocks_of(o, d)


    @pl.loop(0, nb, unroll=4)
    def _(c):
        tsend[c] = chain[table[2 * o + 1, c]]

    tswap = remote(tsend, trecv, pair_s.at[2], pair_r.at[2], {"row": o})
    tswap.start()
    for v in range(1, lo):
        gw_near(v).wait_recv()
    for u in range(hi):
        level = grecv[u * lo + my_lo]
        for v in range(1, lo):
            level = level + gnear[v, u].astype(f32)
        gsum[u] = level
        gmid[u] = level.astype(bf16)
    for u in range(1, hi):
        gw_far(u).start()

    @pl.loop(0, cols_n, unroll=4)
    def _(d):
        blocks_of(r, d)

    tswap.wait_recv()

    @pl.loop(0, nb, unroll=4)
    def _(c):
        last = chain[table[2 * r + 1, c]]
        gf[:, pl.ds(pl.multiple_of(c * bs, bs), bs)] = (last + trecv[c]).astype(bf16)

    total = gsum[my_hi]
    for u in range(1, hi):
        gw_far(u).wait_recv()
        total = total + gfar[u].astype(f32)
    ghalf[...] = total
    gw[rows(r, h), :] = total
    rswap = remote(ghalf, grow, pair_s.at[3], pair_r.at[3], {"row": o})
    rswap.start()
    rswap.wait_recv()
    gw[rows(o, h), :] = grow[...]

    bulk(sout, out_s, out_r).wait_recv()
    own_out.wait()

    bulk(cotf, cot_s, cot_r).wait_send()
    bulk(aggf, agg_s, agg_r).wait_send()
    bulk(sdag, dag_s, dag_r).wait_send()
    bulk(sout, out_s, out_r).wait_send()
    half_copy(r).wait_send()
    for u in range(hi):
        for v in range(1, lo):
            w_near(u, v, origin(u, 0)).wait_send()
    for u in range(1, hi):
        w_far(u, me).wait_send()
        gw_far(u).wait_send()
    for v in range(1, lo):
        gw_near(v).wait_send()
    swap.wait_send()
    gswap.wait_send()
    tswap.wait_send()
    rswap.wait_send()


def fused(cols_n, features, a_blocks, block_cols, block_counts, weight, cotangent):
    fd, n = features.shape
    nb, sections, slots, bs, _ = a_blocks.shape
    full = weight.shape[1]
    npd = n // cols_n
    h = fd // 2
    lo = math.gcd(cols_n, 4)
    hi = cols_n // lo
    scale = 1.0 / math.sqrt(n * sections)
    hbm = pl.BlockSpec(memory_space=pl.ANY)
    vmem = pl.BlockSpec(memory_space=pltpu.VMEM)
    dma = pltpu.SemaphoreType.DMA
    flops = 2 * fd * n * bs * sections * slots * 2 + 6 * full * full * npd
    results = pl.pallas_call(
        functools.partial(kernel, cols_n, scale),
        out_shape=(
            jax.ShapeDtypeStruct((fd, n), bf16),
            jax.ShapeDtypeStruct((fd, full), f32),
            jax.ShapeDtypeStruct((fd, n), bf16),
        ),
        in_specs=[pl.BlockSpec(memory_space=pltpu.SMEM)] * 2 + [hbm] * 4,
        out_specs=(hbm, vmem, vmem),
        scratch_shapes=[
            pltpu.VMEM(a_blocks.shape, bf16),
            pltpu.VMEM((2, fd, n), bf16),
            pltpu.VMEM((2, n // bs, fd, bs), bf16),
            pltpu.VMEM((nb, fd, bs), f32),
            pltpu.VMEM((cols_n, fd, npd), bf16),
            pltpu.VMEM((full, npd), bf16),
            pltpu.VMEM((2, cols_n, h, full), bf16),
            pltpu.VMEM((full, full), bf16),
            pltpu.VMEM((full, full), bf16),
            pltpu.VMEM((full, npd), bf16),
            pltpu.VMEM((full, npd), bf16),
            pltpu.VMEM((full, npd), bf16),
            pltpu.VMEM((full, npd), bf16),
            pltpu.VMEM((fd, n), bf16),
            pltpu.VMEM((cols_n, 2, h, full), f32),
            pltpu.VMEM((cols_n, h, full), f32),
            pltpu.VMEM((hi, lo, h, full), bf16),
            pltpu.VMEM((lo, hi, h, full), bf16),
            pltpu.VMEM((hi, h, full), f32),
            pltpu.VMEM((hi, h, full), bf16),
            pltpu.VMEM((hi, h, full), bf16),
            pltpu.VMEM((h, full), f32),
            pltpu.VMEM((h, full), f32),
            pltpu.VMEM((nb * slots + 1, fd, bs), f32),
            pltpu.VMEM((nb, fd, bs), f32),
            pltpu.VMEM((nb, fd, bs), f32),
            pltpu.VMEM((8, 128), jnp.int32),
            pltpu.SMEM((8, 128), jnp.int32),
            dma((7,)),
        ] + [dma((cols_n,))] * 14 + [dma((lo,))] * 2 + [dma((hi, lo))] * 2 + [dma((4,))] * 2,
        compiler_params=pltpu.CompilerParams(
            collective_id=0, has_side_effects=True, vmem_limit_bytes=62 * 2**20
        ),
        cost_estimate=pl.CostEstimate(
            flops=flops, bytes_accessed=a_blocks.size * 2 + 8 * fd * n,
            transcendentals=full * npd,
        ),
    )(jnp.transpose(block_cols, (1, 2, 0)), block_counts.T, features, a_blocks, weight, cotangent)
    return pl.pallas_call(
        place,
        out_shape=tuple(jax.ShapeDtypeStruct(x.shape, x.dtype) for x in results),
        in_specs=[hbm] * 3,
        out_specs=(hbm,) * 3,
        scratch_shapes=[pltpu.VMEM(x.shape, x.dtype) for x in results] + [dma((3, 2))],
        compiler_params=pltpu.CompilerParams(vmem_limit_bytes=62 * 2**20),
        cost_estimate=pl.CostEstimate(
            flops=0, bytes_accessed=8 * fd * n + 8 * fd * full, transcendentals=0
        ),
    )(*results)


def place(*refs):
    sems = refs[9]
    into = [pltpu.make_async_copy(refs[i], refs[i + 6], sems.at[i, 0]) for i in range(3)]
    back = [pltpu.make_async_copy(refs[i + 6], refs[i + 3], sems.at[i, 1]) for i in range(3)]
    for copy in into:
        copy.start()
    for i in range(3):
        into[i].wait()
        back[i].start()
    for copy in back:
        copy.wait()


def local(rows_n, cols_n, features, a_blocks, block_cols, block_counts, weight, cotangent):
    fd, n = features.shape
    bs = a_blocks.shape[-1]
    args = (features, a_blocks, block_cols, block_counts, weight, cotangent)
    fits = (
        rows_n == 2
        and a_blocks.shape[1] == 2
        and a_blocks.shape[0] * bs == n
        and bs % 128 == 0
        and n % (cols_n * bs) == 0
        and fd % 32 == 0
        and a_blocks.shape[0] * a_blocks.shape[2] <= 128
        and a_blocks.shape[0] <= 128
        and 128 % fd == 0
        and weight.shape[1] % 128 == 0
        and cols_n % 4 == 0
        and weight.shape[1] == fd * cols_n
    )
    return fused(cols_n, *args) if fits else plain(*args)


def solution(mesh):
    placed = (
        P("col", "row"),
        P("row", None, None, None, None),
        P("row", None, None),
        P("row", None),
        P("col", None),
        P("col", "row"),
    )
    return jax.shard_map(
        functools.partial(local, mesh.shape["row"], mesh.shape["col"]),
        mesh=mesh,
        in_specs=placed,
        out_specs=(P("col", "row"), P("col", None), P("col", "row")),
        check_vma=False,
    )
```

```python
import functools
import math

import jax
import jax.numpy as jnp
from jax import lax
from jax.experimental import pallas as pl
from jax.experimental.pallas import tpu as pltpu
from jax.sharding import PartitionSpec as P

MESH = pl.DeviceIdType.MESH
f32 = jnp.float32
bf16 = jnp.bfloat16


def from_root(value, axis, source):
    kept = jnp.where(lax.axis_index(axis) == source, value, 0).astype(value.dtype)
    return lax.psum(kept, axis)


def plain(features, a_blocks, block_cols, block_counts, weight, cotangent):
    feat_dev = features.shape[0]
    slab_rows = features.shape[1]
    block_size = a_blocks.shape[-1]
    local_blocks = a_blocks.shape[0]
    section_count = a_blocks.shape[1]
    slot_count = a_blocks.shape[2]
    row_blocks = slab_rows // block_size
    slot_ids = jnp.arange(slot_count, dtype=jnp.int32)
    live_mask = (slot_ids[None, None, :] < block_counts[:, :, None]).astype(jnp.bfloat16)
    masked = a_blocks * live_mask[:, :, :, None, None]
    global_index = (
        jnp.arange(section_count, dtype=jnp.int32)[None, :, None] * row_blocks + block_cols
    )
    node_total = slab_rows * lax.axis_size("row")
    total = jnp.zeros((feat_dev, local_blocks, block_size), jnp.float32)
    for section_idx in range(lax.axis_size("row")):
        panel_rows = from_root(features, "row", section_idx).reshape(
            feat_dev, row_blocks, block_size
        )
        picked = panel_rows[:, block_cols[:, section_idx, :]]
        total = total + jnp.einsum(
            "fbkj,bkij->fbi", picked, masked[:, section_idx], preferred_element_type=jnp.float32
        )
    aggregated = total.reshape(feat_dev, slab_rows).astype(jnp.bfloat16)
    agg_full = lax.all_gather(aggregated, "col", axis=0, tiled=True)
    preact = jnp.dot(weight, agg_full, preferred_element_type=jnp.float32)
    output = jax.nn.silu(preact).astype(jnp.bfloat16)
    sigmoid_pre = jax.nn.sigmoid(preact)
    dpre = (
        cotangent.astype(jnp.float32) * sigmoid_pre * (1.0 + preact * (1.0 - sigmoid_pre))
    ).astype(jnp.bfloat16)
    local_grad = lax.dot_general(
        dpre, agg_full, (((1,), (1,)), ((), ())), preferred_element_type=jnp.float32
    )
    grad_weight = lax.psum(local_grad, "row") / jnp.sqrt(jnp.float32(node_total))
    dpre_full, weight_full = (
        lax.all_gather(dpre, "col", axis=0, tiled=True),
        lax.all_gather(weight, "col", axis=0, tiled=True),
    )
    first_col = lax.axis_index("col") * feat_dev
    weight_cols = lax.dynamic_slice_in_dim(weight_full, first_col, feat_dev, 1)
    dagg = lax.dot_general(
        weight_cols, dpre_full, (((0,), (0,)), ((), ())), preferred_element_type=jnp.float32
    ).astype(jnp.bfloat16)
    contrib = jnp.einsum(
        "fbi,bskij->fbskj",
        dagg.reshape(feat_dev, local_blocks, block_size),
        masked,
        preferred_element_type=jnp.float32,
    )
    terms = (
        jnp.zeros((feat_dev, section_count * row_blocks, block_size), jnp.float32)
        .at[:, global_index]
        .add(contrib)
    )
    terms = terms.reshape(feat_dev, section_count * slab_rows)
    grad_features = lax.psum_scatter(terms, "row", scatter_dimension=1, tiled=True).astype(
        jnp.bfloat16
    )
    return (output, grad_weight, grad_features)


NT = (((1,), (1,)), ((), ()))


def link_rows(block_cols, s, order, slots):
    lane = lax.broadcasted_iota(jnp.int32, (1, 128), 1)
    dest = jnp.full((1, 128), -1, jnp.int32)
    for i, b in enumerate(order):
        for k in range(slots):
            dest = jnp.where(lane == i * slots + k, block_cols[s, k, b], dest)
    across = jnp.broadcast_to(dest, (128, 128))
    down = across.T
    first = lax.broadcasted_iota(jnp.int32, (128, 128), 0)
    second = lax.broadcasted_iota(jnp.int32, (128, 128), 1)
    before = jnp.where((down == across) & (first < second), first + 1, 0)
    last = jnp.where(down == second, first + 1, 0)
    return jnp.max(before, axis=0, keepdims=True), jnp.max(last, axis=0, keepdims=True)


def kernel(
    cols_n, scale,
    block_cols, counts, feat, a, w, cot,
    out, gw, gf,
    av, fv, fb, acc, sagg, aggf, wh, wf, wt, cotf, dpre, sout, sdag, rdag,
    gpart, grecv, gsend, gnear, gsum, gmid, gfar, grow, ghalf, chain, tsend, trecv, table_v, table,
    loc, cot_s, cot_r, w_s, w_r, wf_s, wf_r, agg_s, agg_r, out_s, out_r,
    dag_s, dag_r, gw_s, gw_r, gn_s, gn_r, wn_s, wn_r, pair_s, pair_r,
):
    me = lax.axis_index("col")
    r = lax.axis_index("row")
    o = 1 - r
    fd, n = feat.shape
    nb, sections, slots, bs, _ = a.shape
    full = wf.shape[0]
    npd = n // cols_n
    bpd = npd // bs
    h = fd // 2
    entries = nb * slots
    chunk = math.gcd(full, 128)

    def peer(d):
        return lax.rem(me + d, cols_n)

    def source(d):
        return lax.rem(me + cols_n - d, cols_n)

    def rows(c, size):
        return pl.ds(pl.multiple_of(c * size, size), size)

    def remote(src, dst, ss, rs, where):
        return pltpu.make_async_remote_copy(
            src_ref=src, dst_ref=dst, send_sem=ss, recv_sem=rs,
            device_id=where, device_id_type=MESH,
        )

    def each(fn):
        @pl.loop(1, cols_n)
        def _(d):
            fn(d)

    barrier = pltpu.get_barrier_semaphore()
    pl.semaphore_signal(barrier, inc=1, device_id={"row": o}, device_id_type=MESH)
    each(lambda d: pl.semaphore_signal(
        barrier, inc=1, device_id={"col": peer(d)}, device_id_type=MESH))

    own_feat = pltpu.make_async_copy(feat, fv.at[r], loc.at[0])
    own_a = pltpu.make_async_copy(a.at[:, r], av.at[:, r], loc.at[1])
    other_a = pltpu.make_async_copy(a.at[:, o], av.at[:, o], loc.at[2])
    own_w = pltpu.make_async_copy(w.at[rows(r, h)], wh.at[r, me], loc.at[3])
    own_cot = pltpu.make_async_copy(cot.at[:, rows(me, npd)], cotf.at[rows(me, fd)], loc.at[4])
    own_feat.start()
    own_a.start()
    other_a.start()
    own_w.start()
    own_cot.start()
    pl.semaphore_wait(barrier, cols_n)

    swap = remote(feat, fv.at[r], pair_s.at[0], pair_r.at[0], {"row": o})
    swap_in = remote(feat, fv.at[o], pair_s.at[0], pair_r.at[0], {"row": o})
    swap.start()

    lo = math.gcd(cols_n, 4)
    hi = cols_n // lo
    my_lo = lax.rem(me, lo)
    my_hi = me // lo

    def near(v):
        return my_hi * lo + lax.rem(my_lo + v, lo)

    def far(u):
        return lax.rem(my_hi + u, hi) * lo + my_lo

    def origin(u, v):
        return lax.rem(my_hi + hi - u, hi) * lo + lax.rem(my_lo + lo - v, lo)

    def w_far(u, c):
        return remote(w.at[rows(r, h)], wh.at[r, c], w_s.at[u], w_r.at[u],
                      {"col": far(u)})

    def w_near(u, v, c):
        part = wh.at[r, c]
        return remote(part, part, wn_s.at[u, v], wn_r.at[u, v], {"col": near(v)})

    def cot_copy(d, c):
        return remote(cot.at[:, rows(peer(d), npd)], cotf.at[rows(c, fd)], cot_s.at[0],
                      cot_r.at[0], {"col": peer(d)})

    def bulk(ref, ss, rs):
        part = ref.at[pl.ds(0, (cols_n - 1) * fd)]
        return remote(part, part, ss.at[0], rs.at[0], {"row": o})

    def half_copy(half):
        return remote(wh.at[half], wh.at[half], wf_s.at[0], wf_r.at[0], {"row": o})

    def agg_copy(d, c):
        return remote(sagg.at[peer(d)], aggf.at[rows(c, fd)], agg_s.at[0], agg_r.at[0],
                      {"col": peer(d)})

    def out_copy(d, c):
        return remote(sout.at[rows(peer(d), fd)], out.at[:, rows(c, npd)], out_s.at[0],
                      out_r.at[0], {"col": peer(d)})

    def dag_copy(d, c):
        return remote(sdag.at[rows(peer(d), fd)], rdag.at[:, rows(c, npd)], dag_s.at[0],
                      dag_r.at[d], {"col": peer(d)})

    def gw_near(v):
        return remote(gsend.at[:, lax.rem(my_lo + v, lo)], gnear.at[v], gn_s.at[v], gn_r.at[v],
                      {"col": near(v)})

    def gw_far(u):
        return remote(gmid.at[lax.rem(my_hi + u, hi)], gfar.at[u], gw_s.at[u], gw_r.at[u],
                      {"col": far(u)})

    for u in range(1, hi):
        w_far(u, me).start()
    own_w.wait()
    for v in range(1, lo):
        w_near(0, v, me).start()
    each(lambda d: cot_copy(d, me).start())

    def alive(count, k):
        return jnp.minimum(jnp.maximum(count - k, 0), 1).astype(f32)

    def split_blocks(s):
        for c in range(nb):
            fb[s, c] = fv[s, :, c * bs:(c + 1) * bs]

    def gathered(b, s):
        picks = []
        count = counts[s, b]
        for k in range(slots):
            c = block_cols[s, k, b]
            picks.append((fb[s, c].astype(f32) * alive(count, k)).astype(bf16))
        left = jnp.concatenate(picks, axis=1)
        right = jnp.concatenate([av[b, s, k] for k in range(slots)], axis=1)
        return lax.dot_general(left, right, NT, preferred_element_type=f32)

    own_feat.wait()
    split_blocks(r)
    own_a.wait()

    @pl.loop(0, nb, unroll=4)
    def _(b):
        acc[b] = gathered(b, r)

    for u in range(1, hi):
        w_far(u, origin(u, 0)).wait_recv()
        for v in range(1, lo):
            w_near(u, v, origin(u, 0)).start()

    swap_in.wait_recv()
    split_blocks(o)
    other_a.wait()

    def finish(c):
        parts = []
        for j in range(bpd):
            b = c * bpd + j
            parts.append((acc[b] + gathered(b, o)).astype(bf16))
        return jnp.concatenate(parts, axis=1)

    def send_agg(d):
        sagg[peer(d)] = finish(peer(d))
        agg_copy(d, me).start()

    pl.loop(1, cols_n, unroll=3)(send_agg)
    aggf[rows(me, fd), :] = finish(me)

    for d in range(1, cols_n):
        u, v = d // lo, d % lo
        if v:
            w_near(u, v, origin(u, v)).wait_recv()
    half_copy(r).start()
    order = [source(d) * bpd + j for d in range(cols_n) for j in range(bpd)]
    for s in range(sections):
        by_entry, by_block = link_rows(block_cols, s, order, slots)
        table_v[2 * s:2 * s + 1, :] = by_entry
        table_v[2 * s + 1:2 * s + 2, :] = by_block
    put_table = pltpu.make_async_copy(table_v, table, loc.at[6])
    put_table.start()
    half_copy(o).wait_recv()
    for c in range(cols_n):
        for half in range(2):
            wf[pl.ds(c * fd + half * h, h), :] = wh[half, c]
    for q in range(full // chunk):
        wt[:, pl.ds(q * chunk, chunk)] = wf[pl.ds(q * chunk, chunk), :].T
    own_cot.wait()
    bulk(cotf, cot_s, cot_r).wait_recv()
    bulk(aggf, agg_s, agg_r).wait_recv()

    for q in range(full // chunk):
        at = pl.ds(q * chunk, chunk)
        pre = jnp.dot(wf[at, :], aggf[...], preferred_element_type=f32)
        sig = jax.nn.sigmoid(pre)
        sout[at, :] = (pre * sig).astype(bf16)
        dpre[at, :] = (cotf[at, :].astype(f32) * sig * (1.0 + pre * (1.0 - sig))).astype(bf16)
    for q in range(full // chunk):
        at = pl.ds(q * chunk, chunk)
        sdag[at, :] = jnp.dot(wt[at, :], dpre[...], preferred_element_type=f32).astype(bf16)

    each(lambda d: dag_copy(d, me).start())
    each(lambda d: out_copy(d, me).start())
    rdag[:, rows(me, npd)] = sdag[rows(me, fd), :]
    own_out = pltpu.make_async_copy(sout.at[rows(me, fd)], out.at[:, rows(me, npd)], loc.at[5])
    own_out.start()

    per_chunk = chunk // fd
    for q in range(full // chunk):
        part = lax.dot_general(dpre[pl.ds(q * chunk, chunk), :], aggf[...], NT,
                               preferred_element_type=f32) * scale
        gpart[pl.ds(q * per_chunk, per_chunk)] = part.reshape(per_chunk, 2, h, full)
    gswap = remote(gpart.at[:, o], grecv, pair_s.at[1], pair_r.at[1], {"row": o})
    gswap.start()
    gswap.wait_recv()

    @pl.loop(0, cols_n)
    def _(c):
        both = gpart[c, r] + grecv[c]
        grecv[c] = both
        gsend[c // lo, lax.rem(c, lo)] = both.astype(bf16)

    for v in range(1, lo):
        gw_near(v).start()

    put_table.wait()
    chain[0] = jnp.zeros(chain.shape[1:], f32)

    def blocks_of(s, d):
        for j in range(bpd):
            i = d * bpd + j
            b = source(d) * bpd + j
            count = counts[s, b]
            right = jnp.concatenate([av[b, s, k] for k in range(slots)], axis=1)
            terms = jnp.dot(rdag[:, pl.ds(pl.multiple_of(b * bs, bs), bs)], right,
                            preferred_element_type=f32)
            for k in range(slots):
                e = i * slots + k
                before = chain[table[2 * s, e]]
                chain[e + 1] = before + terms[:, k * bs:(k + 1) * bs] * alive(count, k)

    blocks_of(o, 0)

    @pl.loop(1, cols_n, unroll=3)
    def _(d):
        dag_copy(d, source(d)).wait_recv()
        blocks_of(o, d)


    @pl.loop(0, nb, unroll=4)
    def _(c):
        tsend[c] = chain[table[2 * o + 1, c]]

    tswap = remote(tsend, trecv, pair_s.at[2], pair_r.at[2], {"row": o})
    tswap.start()
    for v in range(1, lo):
        gw_near(v).wait_recv()
    for u in range(hi):
        level = grecv[u * lo + my_lo]
        for v in range(1, lo):
            level = level + gnear[v, u].astype(f32)
        gsum[u] = level
        gmid[u] = level.astype(bf16)
    for u in range(1, hi):
        gw_far(u).start()

    @pl.loop(0, cols_n, unroll=4)
    def _(d):
        blocks_of(r, d)

    tswap.wait_recv()

    @pl.loop(0, nb, unroll=4)
    def _(c):
        last = chain[table[2 * r + 1, c]]
        gf[:, pl.ds(pl.multiple_of(c * bs, bs), bs)] = (last + trecv[c]).astype(bf16)

    total = gsum[my_hi]
    for u in range(1, hi):
        gw_far(u).wait_recv()
        total = total + gfar[u].astype(f32)
    ghalf[...] = total
    gw[rows(r, h), :] = total
    rswap = remote(ghalf, grow, pair_s.at[3], pair_r.at[3], {"row": o})
    rswap.start()
    rswap.wait_recv()
    gw[rows(o, h), :] = grow[...]

    bulk(sout, out_s, out_r).wait_recv()
    own_out.wait()

    bulk(cotf, cot_s, cot_r).wait_send()
    bulk(aggf, agg_s, agg_r).wait_send()
    bulk(sdag, dag_s, dag_r).wait_send()
    bulk(sout, out_s, out_r).wait_send()
    half_copy(r).wait_send()
    for u in range(hi):
        for v in range(1, lo):
            w_near(u, v, origin(u, 0)).wait_send()
    for u in range(1, hi):
        w_far(u, me).wait_send()
        gw_far(u).wait_send()
    for v in range(1, lo):
        gw_near(v).wait_send()
    swap.wait_send()
    gswap.wait_send()
    tswap.wait_send()
    rswap.wait_send()


def fused(cols_n, features, a_blocks, block_cols, block_counts, weight, cotangent):
    fd, n = features.shape
    nb, sections, slots, bs, _ = a_blocks.shape
    full = weight.shape[1]
    npd = n // cols_n
    h = fd // 2
    lo = math.gcd(cols_n, 4)
    hi = cols_n // lo
    scale = 1.0 / math.sqrt(n * sections)
    hbm = pl.BlockSpec(memory_space=pl.ANY)
    vmem = pl.BlockSpec(memory_space=pltpu.VMEM)
    dma = pltpu.SemaphoreType.DMA
    flops = 2 * fd * n * bs * sections * slots * 2 + 6 * full * full * npd
    results = pl.pallas_call(
        functools.partial(kernel, cols_n, scale),
        out_shape=(
            jax.ShapeDtypeStruct((fd, n), bf16),
            jax.ShapeDtypeStruct((fd, full), f32),
            jax.ShapeDtypeStruct((fd, n), bf16),
        ),
        in_specs=[pl.BlockSpec(memory_space=pltpu.SMEM)] * 2 + [hbm] * 4,
        out_specs=(hbm, vmem, vmem),
        scratch_shapes=[
            pltpu.VMEM(a_blocks.shape, bf16),
            pltpu.VMEM((2, fd, n), bf16),
            pltpu.VMEM((2, n // bs, fd, bs), bf16),
            pltpu.VMEM((nb, fd, bs), f32),
            pltpu.VMEM((cols_n, fd, npd), bf16),
            pltpu.VMEM((full, npd), bf16),
            pltpu.VMEM((2, cols_n, h, full), bf16),
            pltpu.VMEM((full, full), bf16),
            pltpu.VMEM((full, full), bf16),
            pltpu.VMEM((full, npd), bf16),
            pltpu.VMEM((full, npd), bf16),
            pltpu.VMEM((full, npd), bf16),
            pltpu.VMEM((full, npd), bf16),
            pltpu.VMEM((fd, n), bf16),
            pltpu.VMEM((cols_n, 2, h, full), f32),
            pltpu.VMEM((cols_n, h, full), f32),
            pltpu.VMEM((hi, lo, h, full), bf16),
            pltpu.VMEM((lo, hi, h, full), bf16),
            pltpu.VMEM((hi, h, full), f32),
            pltpu.VMEM((hi, h, full), bf16),
            pltpu.VMEM((hi, h, full), bf16),
            pltpu.VMEM((h, full), f32),
            pltpu.VMEM((h, full), f32),
            pltpu.VMEM((nb * slots + 1, fd, bs), f32),
            pltpu.VMEM((nb, fd, bs), f32),
            pltpu.VMEM((nb, fd, bs), f32),
            pltpu.VMEM((8, 128), jnp.int32),
            pltpu.SMEM((8, 128), jnp.int32),
            dma((7,)),
        ] + [dma((cols_n,))] * 14 + [dma((lo,))] * 2 + [dma((hi, lo))] * 2 + [dma((4,))] * 2,
        compiler_params=pltpu.CompilerParams(
            collective_id=0, has_side_effects=True, vmem_limit_bytes=62 * 2**20
        ),
        cost_estimate=pl.CostEstimate(
            flops=flops, bytes_accessed=a_blocks.size * 2 + 8 * fd * n,
            transcendentals=full * npd,
        ),
    )(jnp.transpose(block_cols, (1, 2, 0)), block_counts.T, features, a_blocks, weight, cotangent)
    return pl.pallas_call(
        place,
        out_shape=tuple(jax.ShapeDtypeStruct(x.shape, x.dtype) for x in results),
        in_specs=[hbm] * 3,
        out_specs=(hbm,) * 3,
        scratch_shapes=[pltpu.VMEM(x.shape, x.dtype) for x in results] + [dma((3, 2))],
        compiler_params=pltpu.CompilerParams(vmem_limit_bytes=62 * 2**20),
        cost_estimate=pl.CostEstimate(
            flops=0, bytes_accessed=8 * fd * n + 8 * fd * full, transcendentals=0
        ),
    )(*results)


def place(*refs):
    sems = refs[9]
    into = [pltpu.make_async_copy(refs[i], refs[i + 6], sems.at[i, 0]) for i in range(3)]
    back = [pltpu.make_async_copy(refs[i + 6], refs[i + 3], sems.at[i, 1]) for i in range(3)]
    for copy in into:
        copy.start()
    for i in range(3):
        into[i].wait()
        back[i].start()
    for copy in back:
        copy.wait()


def local(rows_n, cols_n, features, a_blocks, block_cols, block_counts, weight, cotangent):
    fd, n = features.shape
    bs = a_blocks.shape[-1]
    args = (features, a_blocks, block_cols, block_counts, weight, cotangent)
    fits = (
        rows_n == 2
        and a_blocks.shape[1] == 2
        and a_blocks.shape[0] * bs == n
        and bs % 128 == 0
        and n % (cols_n * bs) == 0
        and fd % 32 == 0
        and a_blocks.shape[0] * a_blocks.shape[2] <= 128
        and a_blocks.shape[0] <= 128
        and 128 % fd == 0
        and weight.shape[1] % 128 == 0
        and cols_n % 4 == 0
        and weight.shape[1] == fd * cols_n
    )
    return fused(cols_n, *args) if fits else plain(*args)


def solution(mesh):
    placed = (
        P("col", "row"),
        P("row", None, None, None, None),
        P("row", None, None),
        P("row", None),
        P("col", None),
        P("col", "row"),
    )
    return jax.shard_map(
        functools.partial(local, mesh.shape["row"], mesh.shape["col"]),
        mesh=mesh,
        in_specs=placed,
        out_specs=(P("col", "row"), P("col", None), P("col", "row")),
        check_vma=False,
    )
```
